512 devices in a mesh: row: 32 (over y_hi, z), col: 16 (over y_lo, x, core).
Axes of the slice: x: 4, y: 4 (y_hi: 2, y_lo: 2; y = y_hi * 2 + y_lo), z: 16, core: 2. Of those that a mesh axis runs over, the one named last changes fastest.
Arguments:
- pair_rep: bfloat16 [512, 512, 128], P('row', 'col'), may hold values from -6 to 6
- input_gain: float32 [128], replicated, may hold values from 0.5 to 1.5
- input_bias: float32 [128], replicated, may hold values from -3 to 3
- proj_weight: bfloat16 [128, 512], replicated, may hold values from -0.5 to 0.5
- proj_bias: float32 [512], replicated, may hold values from -3 to 3
- norm_gain: float32 [128], replicated, may hold values from 0.5 to 1.5
- norm_bias: float32 [128], replicated, may hold values from -3 to 3
- out_weight: bfloat16 [128, 128], replicated, may hold values from -0.5 to 0.5
- out_bias: float32 [128], replicated, may hold values from -3 to 3
- gate_weight: bfloat16 [128, 128], replicated, may hold values from -0.5 to 0.5
- gate_bias: float32 [128], replicated, may hold values from -3 to 3
Outputs:
- update: bfloat16 [512, 512, 128], P('row', 'col')
The draws below stay inside these ranges and needn't reach their ends.
All inputs are finite; a program needn't handle non-finite values.
Results may differ from the reference program's by a relative error of at most 0.0051.
Values may be sent and summed in bfloat16 or wider, within the bound.
A program may use at most 64 MiB of HBM per device.

```python
import jax
import jax.numpy as jnp
from jax import lax

C = 128
H = 128
N_RES = 512


def level_of(key, dims, pieces, smallest, high):
    level = 1.0
    for position, parts in pieces:
        steps = jax.random.uniform(jax.random.fold_in(jax.random.fold_in(key, 6), position), (parts,), jnp.float32, smallest / len(pieces), high / len(pieces))
        level = level * jnp.repeat(jnp.exp(steps), dims[position] // parts).reshape((-1,) + (1,) * (len(dims) - 1 - position))
    return level


def normal_values(own_key, extent, deviation, reach, pieces=(), held_as=jnp.bfloat16):
    result = deviation * jax.random.normal(own_key, extent, jnp.float32)
    if pieces:
        result = result * level_of(own_key, extent, pieces, -0.22, 0.18)
    return jnp.clip(result, -reach, reach).astype(held_as)


def setup_inputs(seed: int = 0) -> dict:
    arg_keys = jax.random.split(jax.random.key(seed), 12)
    return {
        "pair_rep": normal_values(arg_keys[0], (N_RES, N_RES, C), 1.0, 6.0, ((0, 32), (1, 16))),
        "input_gain": jnp.clip(jax.random.uniform(arg_keys[1], (C,), jnp.float32, 0.5, 1.5), 0.5, 1.5),
        "input_bias": normal_values(arg_keys[2], (C,), 0.5, 3.0, (), jnp.float32),
        "proj_weight": normal_values(arg_keys[3], (C, 4 * H), C ** -0.5, 0.5),
        "proj_bias": normal_values(arg_keys[4], (4 * H,), 0.5, 3.0, (), jnp.float32),
        "norm_gain": jnp.clip(jax.random.uniform(arg_keys[5], (H,), jnp.float32, 0.5, 1.5), 0.5, 1.5),
        "norm_bias": normal_values(arg_keys[6], (H,), 0.5, 3.0, (), jnp.float32),
        "out_weight": normal_values(arg_keys[7], (H, C), H ** -0.5, 0.5),
        "out_bias": normal_values(arg_keys[8], (C,), 0.5, 3.0, (), jnp.float32),
        "gate_weight": normal_values(arg_keys[9], (C, C), C ** -0.5, 0.5),
        "gate_bias": normal_values(arg_keys[10], (C,), 0.5, 3.0, (), jnp.float32),
    }


def layer_norm(values, gain, bias):
    mean = lax.optimization_barrier(jnp.mean(values, axis=-1, keepdims=True))
    centred = values - mean
    var = lax.optimization_barrier(jnp.mean(centred * centred, axis=-1, keepdims=True))
    return centred * jax.lax.rsqrt(var + 1e-05) * gain + bias

def reference(pair_rep, input_gain, input_bias, proj_weight, proj_bias, norm_gain, norm_bias, out_weight, out_bias, gate_weight, gate_bias):
    hidden = norm_gain.shape[0]
    chans = pair_rep.shape[2]
    count = pair_rep.shape[0]
    normed = layer_norm(pair_rep.astype(jnp.float32), input_gain, input_bias).astype(jnp.bfloat16)
    flat = normed.reshape(-1, chans)
    proj = jnp.dot(flat, proj_weight, preferred_element_type=jnp.float32) + proj_bias
    left = (jax.nn.sigmoid(proj[:, :hidden]) * proj[:, hidden:2 * hidden]).astype(jnp.bfloat16)
    right = (jax.nn.sigmoid(proj[:, 2 * hidden:3 * hidden]) * proj[:, 3 * hidden:]).astype(jnp.bfloat16)
    left = left.reshape(count, count, hidden).astype(jnp.float32)
    right = right.reshape(count, count, hidden).astype(jnp.float32)
    joined = jnp.einsum('ikh,jkh->ijh', left, right)
    joined_norm = layer_norm(joined, norm_gain, norm_bias).astype(jnp.bfloat16).reshape(-1, hidden)
    gate = jax.nn.sigmoid(jnp.dot(flat, gate_weight, preferred_element_type=jnp.float32) + gate_bias)
    value = jnp.dot(joined_norm, out_weight, preferred_element_type=jnp.float32) + out_bias
    return (gate * value).astype(jnp.bfloat16).reshape(count, count, chans)
```

```python
import jax
import jax.numpy as jnp
from jax import lax
from jax.experimental import pallas as pl
from jax.experimental.pallas import tpu as pltpu
from jax.sharding import PartitionSpec as P

MESH = pl.DeviceIdType.MESH
F32 = jnp.float32
BF16 = jnp.bfloat16


def dot_nn(a, b):
    return lax.dot_general(a, b, (((1,), (0,)), ((), ())), preferred_element_type=F32)


def dot_nt(a, b):
    return lax.dot_general(a, b, (((1,), (1,)), ((), ())), preferred_element_type=F32)


def iota(shape, dim):
    return lax.broadcasted_iota(jnp.int32, shape, dim)


def eye(n):
    return (iota((n, n), 0) == iota((n, n), 1)).astype(F32).astype(BF16)


def layer_norm_lanes(values, gain, bias):
    mean = jnp.mean(values, axis=-1, keepdims=True)
    centred = values - mean
    var = jnp.mean(centred * centred, axis=-1, keepdims=True)
    return centred * lax.rsqrt(var + 1e-05) * gain + bias


def sigmoid(x):
    return 1.0 / (1.0 + jnp.exp(-x))


def project(pair, gain, bias, proj_w, proj_b):
    normed = layer_norm_lanes(pair.astype(F32), gain, bias).astype(BF16)
    proj = dot_nn(normed, proj_w) + proj_b
    left = (sigmoid(proj[:, :128]) * proj[:, 128:256]).astype(BF16)
    right = (sigmoid(proj[:, 256:384]) * proj[:, 384:]).astype(BF16)
    return normed, left, right


def interleave(parts, roll):
    parts = [p.reshape(16, 8, p.shape[-1]) for p in parts]
    turned = [roll(p, 4, 1) for p in parts]
    low = iota(parts[0].shape, 1) < 4
    even = [jnp.where(low, parts[a], turned[a + 1]) for a in (0, 2)]
    odd = [jnp.where(low, turned[a], parts[a + 1]) for a in (0, 2)]
    return jnp.concatenate(even, axis=1), jnp.concatenate(odd, axis=1)


def edges_out(edge, roll):
    turned = dot_nt(eye(128), edge)
    even, odd = interleave([turned[:, q * 128 : (q + 1) * 128] for q in range(4)], roll)
    return even.astype(BF16), odd.astype(BF16)


def relay(rows):
    return dot_nt(eye(128), rows).astype(BF16).reshape(4, 32, rows.shape[0])


def place_const():
    a, b = iota((512, 256), 0), iota((512, 256), 1)
    j4, c, zhi, rest = a // 128, (a // 64) % 2, (a // 32) % 2, a % 32
    goal = zhi * 128 + j4 * 32 + rest
    return [jnp.where((goal == b) & (c == core), 1.0, 0.0).astype(BF16) for core in range(2)]


def gather_const():
    a, b = iota((1024, 256), 0), iota((1024, 256), 1)
    i4, core, j4, zlo, q = a // 256, (a // 128) % 2, (a // 32) % 4, (a // 16) % 2, (a // 4) % 4
    goal = core * 128 + i4 * 32 + zlo * 16 + q * 4 + j4
    return jnp.where(goal == b, 1.0, 0.0).astype(BF16)


def right_operand(r_all, place):
    cat = jnp.concatenate([r_all[:, j].reshape(256, 128) for j in range(4)], axis=1)
    return jnp.concatenate([dot_nn(cat, place[c]).astype(BF16) for c in range(2)], axis=0)


def join(left, right, gather):
    keep = iota((256, 256), 0) % 4 == iota((256, 256), 1) % 4
    parts = []
    for block in left:
        both = lax.dot_general(block, right, (((0,), (0,)), ((), ())), preferred_element_type=F32)
        parts.append(jnp.where(keep, both, 0.0).astype(BF16))
    return dot_nn(jnp.concatenate(parts, axis=1), gather).astype(BF16)


def group_sum(x, roll):
    row = iota(x.shape, 0)
    x = x + jnp.where(row % 2 == 0, roll(x, 15, 0), roll(x, 1, 0))
    return x + jnp.where(row % 4 < 2, roll(x, 14, 0), roll(x, 2, 0))


def spread(value, roll):
    even, odd = interleave([value] * 4, roll)
    return jnp.stack([even, odd], axis=1).reshape(512, value.shape[-1])


def wide_weight(out_w, roll):
    rows = spread(out_w.astype(F32), roll)
    q = (iota(rows.shape, 0) // 4) % 4
    return jnp.concatenate([jnp.where(q == p, rows, 0.0) for p in range(4)], axis=1).astype(BF16)


def finish(joined, gain, bias, wide, out_b, roll):
    vals = joined.astype(F32).reshape(32, 16, 128)
    mean = group_sum(jnp.sum(vals, axis=0), roll) * (1.0 / 128)
    centred = vals - mean[None]
    var = group_sum(jnp.sum(centred * centred, axis=0), roll) * (1.0 / 128)
    scale = lax.rsqrt(var + 1e-05)
    normed = (centred * scale[None]).reshape(512, 128) * gain + bias
    turned = dot_nt(eye(128), normed.astype(BF16)).astype(BF16)
    value = dot_nn(turned, wide)
    return [value[:, q * 128 : (q + 1) * 128] + out_b for q in range(4)]


def kernel(
    pair_ref, in_gain, in_bias, proj_w, proj_b, norm_gain, norm_bias, out_w, out_b, gate_w, gate_b,
    out_ref,
    x_tx, x_rx, l_all, r_tx, r_all, t_tx, f_rx, gate_s, place_s, gather_s, wide_s, gain_s, bias_s,
    x_send, x_recv, l_send, l_recv, r_send, r_recv, f_send, f_recv,
):
    roll = pltpu.roll
    row, col = lax.axis_index("row"), lax.axis_index("col")
    y_hi, z = row // 16, row % 16
    y_lo, x, core = col // 8, (col // 2) % 4, col % 2
    chip = y_lo * 4 + x
    me = z * 2 + core

    barrier = pltpu.get_barrier_semaphore()

    def greet(device):
        pl.semaphore_signal(barrier, inc=1, device_id=device, device_id_type=MESH)

    def column(t):
        d = (me + t) % 32
        return d, (y_hi * 16 + d // 2, chip * 2 + d % 2)

    @pl.loop(1, 32)
    def _(t):
        greet(column(t)[1])

    here = y_hi * 8 + chip

    @pl.loop(1, 16)
    def _(t):
        p = (here + t) % 16
        greet(((p // 8) * 16 + z, (p % 8) * 2 + core))

    normed, left, right = project(
        pair_ref[...].reshape(512, 128), in_gain[...], in_bias[...], proj_w[...], proj_b[...]
    )
    for side, edge in enumerate((left, right)):
        even, odd = edges_out(edge, roll)
        even, odd = even.reshape(16, 1, 16, 128), odd.reshape(16, 1, 16, 128)
        x_tx[:, side] = jnp.concatenate([even, odd], axis=1)

    pl.semaphore_wait(barrier, 46)

    def edge_copy(d, device):
        return pltpu.make_async_remote_copy(
            src_ref=x_tx.at[d // 2, :, d % 2], dst_ref=x_rx.at[:, me], send_sem=x_send, recv_sem=x_recv,
            device_id=device, device_id_type=MESH,
        )

    @pl.loop(1, 32)
    def _(t):
        d, device = column(t)
        edge_copy(d, device).start()

    own = pltpu.make_async_copy(x_tx.at[z, :, core], x_rx.at[:, me], x_recv)
    own.start()

    gate_s[...] = sigmoid(dot_nn(normed, gate_w[...]) + gate_b[...])
    place = place_const()
    place_s[0], place_s[1] = place[0], place[1]
    gather_s[...] = gather_const()
    wide_s[...] = wide_weight(out_w[...], roll)
    gain_s[...] = spread(jnp.transpose(jnp.broadcast_to(norm_gain[...], (128, 128))), roll)
    bias_s[...] = spread(jnp.transpose(jnp.broadcast_to(norm_bias[...], (128, 128))), roll)

    pltpu.make_async_copy(x_rx, x_rx, x_recv).wait()

    got = x_rx[...].reshape(2, 16, 2, 16, 128)
    for c in range(2):
        l_all[:, c, chip] = relay(got[0, :, c].reshape(256, 128))

    def left_copy(t):
        p = (chip + t) % 8
        return pltpu.make_async_remote_copy(
            src_ref=l_all.at[:, :, chip], dst_ref=l_all.at[:, :, chip], send_sem=l_send, recv_sem=l_recv,
            device_id=(row, p * 2 + core), device_id_type=MESH,
        )

    @pl.loop(1, 8)
    def _(t):
        left_copy(t).start()

    for s in range(4):
        rows = jnp.concatenate(
            [got[1, 4 * s : 4 * s + 4, c].reshape(64, 128) for c in range(2)], axis=0
        )
        r_tx[s] = relay(rows)

    def right_copy(s, hi):
        return pltpu.make_async_remote_copy(
            src_ref=r_tx.at[s], dst_ref=r_all.at[chip], send_sem=r_send, recv_sem=r_recv,
            device_id=(hi * 16 + z, y_hi * 8 + s * 2 + core), device_id_type=MESH,
        )

    def is_own(s, hi):
        return (hi == y_hi) & (y_lo == y_hi) & (s == x)

    @pl.loop(0, 8)
    def _(t):
        s, hi = t % 4, t // 4
        same = is_own(s, hi)

        @pl.when(same)
        def _():
            pltpu.make_async_copy(r_tx.at[s], r_all.at[chip], r_recv).start()

        @pl.when(jnp.logical_not(same))
        def _():
            right_copy(s, hi).start()

    pltpu.make_async_copy(r_all, r_all, r_recv).wait()
    operand = right_operand(r_all[...], [place_s[0], place_s[1]])
    seven = l_all.at[:, :, pl.ds(0, 7)]
    pltpu.make_async_copy(seven, seven, l_recv).wait()

    joined = join([l_all[i].reshape(512, 256) for i in range(4)], operand, gather_s[...])
    for c in range(2):
        t_tx[:, c] = joined[:, c * 128 : (c + 1) * 128].reshape(16, 16, 128)

    def back_copy(d, device):
        return pltpu.make_async_remote_copy(
            src_ref=t_tx.at[d // 2, d % 2], dst_ref=f_rx.at[me], send_sem=f_send, recv_sem=f_recv,
            device_id=device, device_id_type=MESH,
        )

    @pl.loop(1, 32)
    def _(t):
        d, device = column(t)
        back_copy(d, device).start()

    pltpu.make_async_copy(t_tx.at[z, core], f_rx.at[me], f_recv).start()
    pltpu.make_async_copy(f_rx, f_rx, f_recv).wait()

    values = finish(f_rx[...].reshape(512, 128), gain_s[...], bias_s[...], wide_s[...], out_b[...], roll)
    for q in range(4):
        update = values[q] * gate_s[q * 128 : (q + 1) * 128]
        out_ref[4 * q : 4 * q + 4] = update.astype(BF16).reshape(4, 32, 128)

    @pl.loop(1, 32)
    def _(t):
        d, device = column(t)
        edge_copy(d, device).wait_send()
        back_copy(d, device).wait_send()

    @pl.loop(1, 8)
    def _(t):
        left_copy(t).wait_send()

    @pl.loop(0, 8)
    def _(t):
        s, hi = t % 4, t // 4

        @pl.when(jnp.logical_not(is_own(s, hi)))
        def _():
            right_copy(s, hi).wait_send()


def per_device(pair, in_gain, in_bias, proj_w, proj_b, norm_gain, norm_bias, out_w, out_b, gate_w, gate_b):
    def flat(v):
        return v.reshape(1, -1)

    vmem = pl.BlockSpec(memory_space=pltpu.VMEM)
    dma = pltpu.SemaphoreType.DMA
    return pl.pallas_call(
        kernel,
        out_shape=jax.ShapeDtypeStruct(pair.shape, BF16),
        in_specs=[vmem] * 11,
        out_specs=vmem,
        scratch_shapes=[
            pltpu.VMEM((16, 2, 2, 16, 128), BF16),
            pltpu.VMEM((2, 32, 16, 128), BF16),
            pltpu.VMEM((4, 2, 8, 32, 256), BF16),
            pltpu.VMEM((4, 4, 32, 128), BF16),
            pltpu.VMEM((8, 4, 32, 128), BF16),
            pltpu.VMEM((16, 2, 16, 128), BF16),
            pltpu.VMEM((32, 16, 128), BF16),
            pltpu.VMEM((512, 128), F32),
            pltpu.VMEM((2, 512, 256), BF16),
            pltpu.VMEM((1024, 256), BF16),
            pltpu.VMEM((512, 512), BF16),
            pltpu.VMEM((512, 128), F32),
            pltpu.VMEM((512, 128), F32),
        ]
        + [dma] * 8,
        compiler_params=pltpu.CompilerParams(
            collective_id=0, has_side_effects=True, vmem_limit_bytes=40 * 1024 * 1024
        ),
    )(
        pair, flat(in_gain), flat(in_bias), proj_w, flat(proj_b), flat(norm_gain), flat(norm_bias),
        out_w, flat(out_b), gate_w, flat(gate_b),
    )


def solution(mesh):
    return jax.shard_map(
        per_device,
        mesh=mesh,
        in_specs=(P("row", "col", None), P(), P(), P(), P(), P(), P(), P(), P(), P(), P()),
        out_specs=P("row", "col", None),
        check_vma=False,
    )
```

```python
import jax
import jax.numpy as jnp
from jax import lax
from jax.experimental import pallas as pl
from jax.experimental.pallas import tpu as pltpu
from jax.sharding import PartitionSpec as P

MESH = pl.DeviceIdType.MESH
F32 = jnp.float32
BF16 = jnp.bfloat16


def dot_nn(a, b):
    return lax.dot_general(a, b, (((1,), (0,)), ((), ())), preferred_element_type=F32)


def dot_nt(a, b):
    return lax.dot_general(a, b, (((1,), (1,)), ((), ())), preferred_element_type=F32)


def iota(shape, dim):
    return lax.broadcasted_iota(jnp.int32, shape, dim)


def eye(n):
    return (iota((n, n), 0) == iota((n, n), 1)).astype(F32).astype(BF16)


def layer_norm_lanes(values, gain, bias):
    mean = jnp.mean(values, axis=-1, keepdims=True)
    centred = values - mean
    var = jnp.mean(centred * centred, axis=-1, keepdims=True)
    return centred * lax.rsqrt(var + 1e-05) * gain + bias


def sigmoid(x):
    return 1.0 / (1.0 + jnp.exp(-x))


def project(pair, gain, bias, proj_w, proj_b):
    normed = layer_norm_lanes(pair.astype(F32), gain, bias).astype(BF16)
    proj = dot_nn(normed, proj_w) + proj_b
    left = (sigmoid(proj[:, :128]) * proj[:, 128:256]).astype(BF16)
    right = (sigmoid(proj[:, 256:384]) * proj[:, 384:]).astype(BF16)
    return normed, left, right


def interleave(parts, roll):
    parts = [p.reshape(16, 8, p.shape[-1]) for p in parts]
    turned = [roll(p, 4, 1) for p in parts]
    low = iota(parts[0].shape, 1) < 4
    even = [jnp.where(low, parts[a], turned[a + 1]) for a in (0, 2)]
    odd = [jnp.where(low, turned[a], parts[a + 1]) for a in (0, 2)]
    return jnp.concatenate(even, axis=1), jnp.concatenate(odd, axis=1)


def edges_out(edge, roll):
    turned = dot_nt(eye(128), edge)
    even, odd = interleave([turned[:, q * 128 : (q + 1) * 128] for q in range(4)], roll)
    return even.astype(BF16), odd.astype(BF16)


def relay_left(rows):
    return dot_nt(eye(128), rows).astype(BF16).reshape(4, 32, 128)


def relay_right(rows):
    twice = jnp.concatenate([rows, rows], axis=0)
    r, c = iota((64, 128), 0), iota((64, 128), 1)
    base = (r // 32) * 64 + r % 32
    halves = [dot_nt(jnp.where(c == base + 32 * p, 1.0, 0.0).astype(BF16), twice) for p in range(2)]
    return jnp.where(c < 64, halves[0], halves[1]).astype(BF16).reshape(2, 32, 128)


def gather_const():
    a, b = iota((1024, 256), 0), iota((1024, 256), 1)
    i4, j4, core, zlo, q = a // 256, (a // 64) % 4, (a // 32) % 2, (a // 16) % 2, (a // 4) % 4
    goal = core * 128 + i4 * 32 + zlo * 16 + q * 4 + j4
    return jnp.where(goal == b, 1.0, 0.0).astype(BF16)


def join(left, right, offset, gather):
    keep = iota((128, 256), 0) % 4 == iota((128, 256), 1) % 4
    offset = jnp.concatenate([offset] * 8, axis=0)
    offset = jnp.concatenate([offset, offset], axis=1)
    parts = []
    for block in left:
        both = lax.dot_general(block, right, (((0,), (0,)), ((), ())), preferred_element_type=F32)
        parts.append(jnp.where(keep, both - offset, 0.0).astype(BF16))
    return dot_nn(jnp.concatenate(parts, axis=1), gather).astype(BF16)


def estimate(in_gain, in_bias, proj_w, proj_b):
    w = proj_w.astype(F32)

    def times(v, m):
        return dot_nn(jnp.concatenate([v] * 8, axis=0), m)[:1]

    mean = times(in_bias, w) + proj_b
    power = in_gain * in_gain
    total = 4.0 * 128.0
    for first in (0, 256):
        g, v = w[:, first : first + 128], w[:, first + 128 : first + 256]
        scale = lax.rsqrt(1.0 + (jnp.pi / 8) * times(power, g * g))
        gate = sigmoid(mean[:, first : first + 128] * scale)
        total = total * (
            gate * mean[:, first + 128 : first + 256] + times(power, g * v) * gate * (1.0 - gate) * scale
        )
    return total


def column(row):
    return jnp.transpose(jnp.broadcast_to(row, (128, 128)))


def group_sum(x, roll):
    row = iota(x.shape, 0)
    x = x + jnp.where(row % 2 == 0, roll(x, 15, 0), roll(x, 1, 0))
    return x + jnp.where(row % 4 < 2, roll(x, 14, 0), roll(x, 2, 0))


def spread(value, roll):
    even, odd = interleave([value] * 4, roll)
    return jnp.stack([even, odd], axis=1).reshape(512, value.shape[-1])


def wide_weight(out_w, roll):
    rows = spread(out_w.astype(F32), roll)
    q = (iota(rows.shape, 0) // 4) % 4
    return jnp.concatenate([jnp.where(q == p, rows, 0.0) for p in range(4)], axis=1).astype(BF16)


def finish(joined, offset, gain, bias, wide, out_b, roll):
    vals = (joined.astype(F32) + offset).reshape(32, 16, 128)
    mean = group_sum(jnp.sum(vals, axis=0), roll) * (1.0 / 128)
    centred = vals - mean[None]
    var = group_sum(jnp.sum(centred * centred, axis=0), roll) * (1.0 / 128)
    scale = lax.rsqrt(var + 1e-05)
    normed = (centred * scale[None]).reshape(512, 128) * gain + bias
    turned = dot_nt(eye(128), normed.astype(BF16)).astype(BF16)
    value = dot_nn(turned, wide)
    return [value[:, q * 128 : (q + 1) * 128] + out_b for q in range(4)]


N_IN = 11
NEAR = (4, 13, 3, 14, 2, 15, 1)
FAR = (8, 7, 9, 6, 10, 5, 11, 12)


def kernel(*refs):
    hbm, out_ref, held, rest = refs[:N_IN], refs[N_IN], refs[N_IN + 1 : 2 * N_IN + 1], refs[2 * N_IN + 1 :]
    pair, in_gain, in_bias, proj_w, proj_b, norm_gain, norm_bias, out_w, out_b, gate_w, gate_b = held
    (
        x_tx, x_rx, y_tx, l_all, r_tx, r_all, t_tx, u_all, f_rx, gate_s, gather_s, wide_s, gain_s, bias_s, off_s,
        in_sem, x_send, x_recv, l_send, l_recv, r_send, r_recv, t_send, t_recv, f_send, f_recv,
    ) = rest
    roll = pltpu.roll
    fetch = [pltpu.make_async_copy(hbm[n], held[n], in_sem.at[n]) for n in range(N_IN)]
    for copy in fetch:
        copy.start()

    row, col = lax.axis_index("row"), lax.axis_index("col")
    y_hi, z = lax.div(row, 16), lax.rem(row, 16)
    y_lo, x, core = lax.div(col, 8), lax.rem(lax.div(col, 2), 4), lax.rem(col, 2)
    barrier = pltpu.get_barrier_semaphore()

    def along_z(off):
        return lax.rem(z + off, 16)

    def greet(device):
        pl.semaphore_signal(barrier, inc=1, device_id=device, device_id_type=MESH)

    for off in FAR + NEAR:
        greet((y_hi * 16 + along_z(off), col))

    @pl.loop(1, 32)
    def _(t):
        p = lax.rem(y_hi * 16 + col + t, 32)
        greet((lax.div(p, 16) * 16 + z, lax.rem(p, 16)))

    for n in range(5):
        fetch[n].wait()
    normed, left, right = project(
        pair[...].reshape(512, 128), in_gain[...], in_bias[...], proj_w[...], proj_b[...]
    )
    for side, edge in enumerate((left, right)):
        even, odd = edges_out(edge, roll)
        x_tx[side] = jnp.concatenate([even.reshape(16, 1, 16, 128), odd.reshape(16, 1, 16, 128)], axis=1)

    pl.semaphore_wait(barrier, 46)

    def edge_copy(side, off):
        there = along_z(off)
        group = 2 if side else int((4 - off) % 16 >= 8)
        slot = z if side else (4 - off) % 16
        return pltpu.make_async_remote_copy(
            src_ref=x_tx.at[side, there], dst_ref=x_rx.at[side, slot], send_sem=x_send,
            recv_sem=x_recv.at[group], device_id=(y_hi * 16 + there, col), device_id_type=MESH,
        )

    pltpu.make_async_copy(x_tx.at[0, z], x_rx.at[0, 4], x_recv.at[0]).start()
    for off in NEAR + FAR:
        edge_copy(0, off).start()
    pltpu.make_async_copy(x_tx.at[1, z], x_rx.at[1, z], x_recv.at[2]).start()
    for off in FAR + NEAR:
        edge_copy(1, off).start()

    for n in range(5, N_IN):
        fetch[n].wait()
    gate_s[...] = sigmoid(dot_nn(normed, gate_w[...]) + gate_b[...])

    def left_copy(group, t):
        p = lax.rem(col + t, 16)
        return pltpu.make_async_remote_copy(
            src_ref=y_tx.at[group, lax.rem(p, 2)], dst_ref=l_all.at[group, col], send_sem=l_send,
            recv_sem=l_recv.at[group], device_id=(row, p), device_id_type=MESH,
        )

    for group in range(2):
        part = x_rx.at[0, pl.ds(8 * group, 8)]
        pltpu.make_async_copy(part, part, x_recv.at[group]).wait()
        for c in range(2):
            y_tx[group, c] = relay_left(x_rx[0, 8 * group : 8 * group + 8, c].reshape(128, 128))
        l_all[group, col] = y_tx[group, core]

        @pl.loop(1, 16)
        def _(t):
            left_copy(group, t).start()

    def right_copy(t):
        s, c, hi = lax.rem(t, 4), lax.rem(lax.div(t, 4), 2), lax.div(t, 8)
        there = (hi * 16 + z, y_hi * 8 + s * 2 + c)
        same = (there[0] == row) & (there[1] == col)
        return same, r_tx.at[s, c], pltpu.make_async_remote_copy(
            src_ref=r_tx.at[s, c], dst_ref=r_all.at[col], send_sem=r_send, recv_sem=r_recv,
            device_id=there, device_id_type=MESH,
        )

    part = x_rx.at[1]
    pltpu.make_async_copy(part, part, x_recv.at[2]).wait()
    for s in range(4):
        for c in range(2):
            r_tx[s, c] = relay_right(x_rx[1, 4 * s : 4 * s + 4, c].reshape(64, 128))

    @pl.loop(0, 16)
    def _(t):
        same, here, copy = right_copy(t)

        @pl.when(same)
        def _():
            pltpu.make_async_copy(here, r_all.at[col], r_recv).start()

        @pl.when(jnp.logical_not(same))
        def _():
            copy.start()

    gather_s[...] = gather_const()
    off_s[...] = spread(column(estimate(in_gain[...], in_bias[...], proj_w[...], proj_b[...])), roll)
    wide_s[...] = wide_weight(out_w[...], roll)
    gain_s[...] = spread(column(norm_gain[...]), roll)
    bias_s[...] = spread(column(norm_bias[...]), roll)
    offset = off_s[pl.ds(pl.multiple_of((z * 2 + core) * 16, 16), 16), :]

    pltpu.make_async_copy(r_all, r_all, r_recv).wait()
    operand = jnp.concatenate([r_all[:, 0].reshape(512, 128), r_all[:, 1].reshape(512, 128)], axis=1)

    def sibling_copy(group):
        return pltpu.make_async_remote_copy(
            src_ref=t_tx.at[group], dst_ref=u_all.at[pl.ds(8 * group, 8), core], send_sem=t_send,
            recv_sem=t_recv.at[group], device_id=(row, col + 1 - 2 * core), device_id_type=MESH,
        )

    def back_copy(off):
        there = along_z(off)
        return pltpu.make_async_remote_copy(
            src_ref=u_all.at[(off + 4) % 16], dst_ref=f_rx.at[z], send_sem=f_send, recv_sem=f_recv,
            device_id=(y_hi * 16 + there, col), device_id_type=MESH,
        )

    for group in range(2):
        part = l_all.at[group, pl.ds(0, 15)]
        pltpu.make_async_copy(part, part, l_recv.at[group]).wait()
        joined = join(
            [l_all[group, :, i].reshape(512, 128) for i in range(4)], operand, offset, gather_s[...]
        ).reshape(8, 16, 256)
        low, high = joined[:, :, :128], joined[:, :, 128:]
        first = core == 0
        t_tx[group] = jnp.where(first, high, low)
        sibling_copy(group).start()
        u_all[8 * group : 8 * group + 8, core] = jnp.where(first, low, high)
        part = u_all.at[pl.ds(8 * group, 8), 1 - core]
        pltpu.make_async_copy(part, part, t_recv.at[group]).wait()
        for off in FAR + NEAR:
            if (off + 4) % 16 // 8 == group:
                back_copy(off).start()
    pltpu.make_async_copy(u_all.at[4], f_rx.at[z], f_recv).start()

    pltpu.make_async_copy(f_rx, f_rx, f_recv).wait()
    values = finish(
        f_rx[...].reshape(512, 128), off_s[...], gain_s[...], bias_s[...], wide_s[...], out_b[...], roll
    )
    for q in range(4):
        update = values[q] * gate_s[q * 128 : (q + 1) * 128]
        out_ref[4 * q : 4 * q + 4] = update.astype(BF16).reshape(4, 32, 128)

    for off in NEAR + FAR:
        edge_copy(0, off).wait_send()
        edge_copy(1, off).wait_send()
        back_copy(off).wait_send()
    for group in range(2):
        sibling_copy(group).wait_send()

        @pl.loop(1, 16)
        def _(t):
            left_copy(group, t).wait_send()

    @pl.loop(0, 16)
    def _(t):
        same, _, copy = right_copy(t)

        @pl.when(jnp.logical_not(same))
        def _():
            copy.wait_send()


def per_device(*args):
    args = [a.reshape(1, -1) if a.ndim == 1 else a for a in args]
    dma = pltpu.SemaphoreType.DMA
    return pl.pallas_call(
        kernel,
        out_shape=jax.ShapeDtypeStruct(args[0].shape, BF16),
        in_specs=[pl.BlockSpec(memory_space=pl.ANY)] * N_IN,
        out_specs=pl.BlockSpec(memory_space=pltpu.VMEM),
        scratch_shapes=[pltpu.VMEM(a.shape, a.dtype) for a in args]
        + [
            pltpu.VMEM((2, 16, 2, 16, 128), BF16),
            pltpu.VMEM((2, 16, 2, 16, 128), BF16),
            pltpu.VMEM((2, 2, 4, 32, 128), BF16),
            pltpu.VMEM((2, 16, 4, 32, 128), BF16),
            pltpu.VMEM((4, 2, 2, 32, 128), BF16),
            pltpu.VMEM((16, 2, 32, 128), BF16),
            pltpu.VMEM((2, 8, 16, 128), BF16),
            pltpu.VMEM((16, 2, 16, 128), BF16),
            pltpu.VMEM((16, 2, 16, 128), BF16),
            pltpu.VMEM((512, 128), F32),
            pltpu.VMEM((1024, 256), BF16),
            pltpu.VMEM((512, 512), BF16),
            pltpu.VMEM((512, 128), F32),
            pltpu.VMEM((512, 128), F32),
            pltpu.VMEM((512, 128), F32),
            dma((N_IN,)), dma, dma((3,)), dma, dma((2,)), dma, dma, dma, dma((2,)), dma, dma,
        ],
        compiler_params=pltpu.CompilerParams(
            collective_id=0, has_side_effects=True, vmem_limit_bytes=56 * 1024 * 1024
        ),
    )(*args)


def solution(mesh):
    return jax.shard_map(
        per_device,
        mesh=mesh,
        in_specs=(P("row", "col", None), P(), P(), P(), P(), P(), P(), P(), P(), P(), P()),
        out_specs=P("row", "col", None),
        check_vma=False,
    )
```

```python
import jax
import jax.numpy as jnp
from jax import lax
from jax.experimental import pallas as pl
from jax.experimental.pallas import tpu as pltpu
from jax.sharding import PartitionSpec as P

MESH = pl.DeviceIdType.MESH
F32 = jnp.float32
BF16 = jnp.bfloat16


def dot_nn(a, b):
    return lax.dot_general(a, b, (((1,), (0,)), ((), ())), preferred_element_type=F32)


def dot_nt(a, b):
    return lax.dot_general(a, b, (((1,), (1,)), ((), ())), preferred_element_type=F32)


def iota(shape, dim):
    return lax.broadcasted_iota(jnp.int32, shape, dim)


def eye(n):
    return (iota((n, n), 0) == iota((n, n), 1)).astype(F32).astype(BF16)


def layer_norm_lanes(values, gain, bias):
    mean = jnp.mean(values, axis=-1, keepdims=True)
    centred = values - mean
    var = jnp.mean(centred * centred, axis=-1, keepdims=True)
    return centred * lax.rsqrt(var + 1e-05) * gain + bias


def sigmoid(x):
    return 1.0 / (1.0 + jnp.exp(-x))


def project(pair, gain, bias, proj_w, proj_b):
    normed = layer_norm_lanes(pair.astype(F32), gain, bias).astype(BF16)
    proj = dot_nn(normed, proj_w) + proj_b
    left = (sigmoid(proj[:, :128]) * proj[:, 128:256]).astype(BF16)
    right = (sigmoid(proj[:, 256:384]) * proj[:, 384:]).astype(BF16)
    return normed, left, right


def interleave(parts, roll):
    parts = [p.reshape(16, 8, p.shape[-1]) for p in parts]
    turned = [roll(p, 4, 1) for p in parts]
    low = iota(parts[0].shape, 1) < 4
    even = [jnp.where(low, parts[a], turned[a + 1]) for a in (0, 2)]
    odd = [jnp.where(low, turned[a], parts[a + 1]) for a in (0, 2)]
    return jnp.concatenate(even, axis=1), jnp.concatenate(odd, axis=1)


def edges_out(edge, roll):
    turned = dot_nt(eye(128), edge)
    even, odd = interleave([turned[:, q * 128 : (q + 1) * 128] for q in range(4)], roll)
    return even.astype(BF16), odd.astype(BF16)


def relay_left(rows):
    return dot_nt(eye(128), rows).astype(BF16).reshape(4, 32, 128)


def relay_right(rows):
    twice = jnp.concatenate([rows, rows], axis=0)
    r, c = iota((64, 128), 0), iota((64, 128), 1)
    base = (r // 32) * 64 + r % 32
    halves = [dot_nt(jnp.where(c == base + 32 * p, 1.0, 0.0).astype(BF16), twice) for p in range(2)]
    return jnp.where(c < 64, halves[0], halves[1]).astype(BF16).reshape(2, 32, 128)


def gather_const():
    a, b = iota((1024, 256), 0), iota((1024, 256), 1)
    i4, j4, core, zlo, q = a // 256, (a // 64) % 4, (a // 32) % 2, (a // 16) % 2, (a // 4) % 4
    goal = core * 128 + i4 * 32 + zlo * 16 + q * 4 + j4
    return jnp.where(goal == b, 1.0, 0.0).astype(BF16)


def join(left, right, gather):
    keep = iota((128, 256), 0) % 4 == iota((128, 256), 1) % 4
    high, low = [], []
    for block in left:
        both = lax.dot_general(block, right, (((0,), (0,)), ((), ())), preferred_element_type=F32)
        both = jnp.where(keep, both, 0.0)
        high.append(both.astype(BF16))
        low.append((both - high[-1].astype(F32)).astype(BF16))
    return dot_nn(jnp.concatenate(high, axis=1), gather) + dot_nn(jnp.concatenate(low, axis=1), gather)


def estimate(in_gain, in_bias, proj_w, proj_b):
    w = proj_w.astype(F32)

    def times(v, m):
        return dot_nn(jnp.concatenate([v] * 8, axis=0), m)[:1]

    mean = times(in_bias, w) + proj_b
    power = in_gain * in_gain
    total = 4.0 * 128.0
    for first in (0, 256):
        g, v = w[:, first : first + 128], w[:, first + 128 : first + 256]
        scale = lax.rsqrt(1.0 + (jnp.pi / 8) * times(power, g * g))
        gate = sigmoid(mean[:, first : first + 128] * scale)
        total = total * (
            gate * mean[:, first + 128 : first + 256] + times(power, g * v) * gate * (1.0 - gate) * scale
        )
    return total


def column(row):
    return jnp.transpose(jnp.broadcast_to(row, (128, 128)))


def group_sum(x, roll):
    row = iota(x.shape, 0)
    x = x + jnp.where(row % 2 == 0, roll(x, 15, 0), roll(x, 1, 0))
    return x + jnp.where(row % 4 < 2, roll(x, 14, 0), roll(x, 2, 0))


def spread(value, roll):
    even, odd = interleave([value] * 4, roll)
    return jnp.stack([even, odd], axis=1).reshape(512, value.shape[-1])


def wide_weight(out_w, roll):
    rows = spread(out_w.astype(F32), roll)
    q = (iota(rows.shape, 0) // 4) % 4
    return jnp.concatenate([jnp.where(q == p, rows, 0.0) for p in range(4)], axis=1).astype(BF16)


def finish(joined, offset, gain, bias, wide, out_b, roll):
    vals = (joined.astype(F32) + offset).reshape(32, 16, 128)
    mean = group_sum(jnp.sum(vals, axis=0), roll) * (1.0 / 128)
    centred = vals - mean[None]
    var = group_sum(jnp.sum(centred * centred, axis=0), roll) * (1.0 / 128)
    scale = lax.rsqrt(var + 1e-05)
    normed = (centred * scale[None]).reshape(512, 128) * gain + bias
    turned = dot_nt(eye(128), normed.astype(BF16)).astype(BF16)
    value = dot_nn(turned, wide)
    return [value[:, q * 128 : (q + 1) * 128] + out_b for q in range(4)]


N_IN = 11
ORDER = (8, 7, 9, 6, 10, 5, 11, 4, 12, 3, 13, 2, 14, 1, 15)


def kernel(*refs):
    hbm, out_ref, held, rest = refs[:N_IN], refs[N_IN], refs[N_IN + 1 : 2 * N_IN + 1], refs[2 * N_IN + 1 :]
    pair, in_gain, in_bias, proj_w, proj_b, norm_gain, norm_bias, out_w, out_b, gate_w, gate_b = held
    (
        x_tx, x_rx, l_all, r_tx, r_all, t_own, t_tx, t_rx, u_all, f_rx, gate_s, gather_s, wide_s, gain_s, bias_s, off_s,
        in_sem, x_send, x_recv, l_send, l_recv, r_send, r_recv, t_send, t_recv, f_send, f_recv,
    ) = rest
    roll = pltpu.roll
    fetch = [pltpu.make_async_copy(hbm[n], held[n], in_sem.at[n]) for n in range(N_IN)]
    for copy in fetch:
        copy.start()

    row, col = lax.axis_index("row"), lax.axis_index("col")
    y_hi, z = lax.div(row, 16), lax.rem(row, 16)
    y_lo, x, core = lax.div(col, 8), lax.rem(lax.div(col, 2), 4), lax.rem(col, 2)
    chip = y_lo * 4 + x
    barrier = pltpu.get_barrier_semaphore()

    def along_z(off):
        return lax.rem(z + off, 16)

    def greet(device):
        pl.semaphore_signal(barrier, inc=1, device_id=device, device_id_type=MESH)

    for off in ORDER:
        greet((y_hi * 16 + along_z(off), col))
    for t in range(1, 16):
        p = lax.rem(y_hi * 8 + chip + t, 16)
        greet((lax.div(p, 8) * 16 + z, lax.rem(p, 8) * 2 + core))
    sibling = (row, col + 1 - 2 * core)
    greet(sibling)

    for n in range(5):
        fetch[n].wait()
    normed, left, right = project(
        pair[...].reshape(512, 128), in_gain[...], in_bias[...], proj_w[...], proj_b[...]
    )
    for side, edge in enumerate((left, right)):
        even, odd = edges_out(edge, roll)
        x_tx[side, 0], x_tx[side, 1] = even, odd

    pl.semaphore_wait(barrier, 31)

    mine = lax.div(z, 8)

    def edge_semaphore(side, c):
        return x_recv.at[side * 4 + (1 - side) * 2 * mine + c]

    def edge_copy(side, c, off):
        there = along_z(off)
        return pltpu.make_async_remote_copy(
            src_ref=x_tx.at[side, c, there], dst_ref=x_rx.at[side, c, z], send_sem=x_send,
            recv_sem=edge_semaphore(side, c), device_id=(y_hi * 16 + there, col), device_id_type=MESH,
        )

    for turn in range(4):
        side = (1 - mine) * (turn % 2) + mine * (1 - turn // 2)
        c = (1 - mine) * (turn // 2) + mine * (turn % 2)
        pltpu.make_async_copy(x_tx.at[side, c, z], x_rx.at[side, c, z], edge_semaphore(side, c)).start()
        for off in ORDER:
            edge_copy(side, c, off).start()

    for n in range(5, N_IN):
        fetch[n].wait()
    gate_s[...] = sigmoid(dot_nn(normed, gate_w[...]) + gate_b[...])
    off_s[...] = spread(column(estimate(in_gain[...], in_bias[...], proj_w[...], proj_b[...])), roll)
    wide_s[...] = wide_weight(out_w[...], roll)
    gain_s[...] = spread(column(norm_gain[...]), roll)
    bias_s[...] = spread(column(norm_bias[...]), roll)
    gather_s[...] = gather_const()

    def left_copy(group, c, p):
        return pltpu.make_async_remote_copy(
            src_ref=l_all.at[group, c, chip], dst_ref=l_all.at[group, c, chip], send_sem=l_send,
            recv_sem=l_recv.at[group, c], device_id=(row, p * 2 + core), device_id_type=MESH,
        )

    def other_chips():
        return [
            lax.rem(y_lo + dy, 2) * 4 + lax.rem(x + dx, 4)
            for dx, dy in ((2, 1), (2, 0), (1, 1), (3, 1), (1, 0), (3, 0), (0, 1))
        ]

    def left_out(group, c):
        part = x_rx.at[0, c, pl.ds(8 * group, 8)]
        pltpu.make_async_copy(part, part, x_recv.at[2 * group + c]).wait()
        l_all[group, c, chip] = relay_left(x_rx[0, c, 8 * group : 8 * group + 8].reshape(128, 128))
        for p in other_chips():
            left_copy(group, c, p).start()

    def right_copy(c, s, hi):
        there = (hi * 16 + z, y_hi * 8 + s * 2 + core)
        same = (there[0] == row) & (there[1] == col)
        return same, pltpu.make_async_remote_copy(
            src_ref=r_tx.at[c, s], dst_ref=r_all.at[c, chip], send_sem=r_send, recv_sem=r_recv.at[c],
            device_id=there, device_id_type=MESH,
        )

    def right_out(c):
        part = x_rx.at[1, c]
        pltpu.make_async_copy(part, part, x_recv.at[4 + c]).wait()
        for s in range(4):
            r_tx[c, s] = relay_right(x_rx[1, c, 4 * s : 4 * s + 4].reshape(64, 128))
        for s in range(4):
            for hi in range(2):
                same, copy = right_copy(c, s, hi)

                @pl.when(same)
                def _():
                    pltpu.make_async_copy(r_tx.at[c, s], r_all.at[c, chip], r_recv.at[c]).start()

                @pl.when(jnp.logical_not(same))
                def _():
                    copy.start()

    def sibling_copy(group, c):
        return pltpu.make_async_remote_copy(
            src_ref=t_tx.at[group, c], dst_ref=t_rx.at[group, c], send_sem=t_send, recv_sem=t_recv.at[group, c],
            device_id=sibling, device_id_type=MESH,
        )

    def back_copy(c, there):
        return pltpu.make_async_remote_copy(
            src_ref=u_all.at[there, c], dst_ref=f_rx.at[z, c], send_sem=f_send, recv_sem=f_recv,
            device_id=(y_hi * 16 + there, col), device_id_type=MESH,
        )

    first = core == 0
    operand = [None, None]

    def product(group, c):
        if operand[c] is None:
            part = r_all.at[c]
            pltpu.make_async_copy(part, part, r_recv.at[c]).wait()
            operand[c] = jnp.concatenate(
                [r_all[c, :, 0].reshape(256, 128), r_all[c, :, 1].reshape(256, 128)], axis=1
            )
        part = l_all.at[group, c, pl.ds(0, 7)]
        pltpu.make_async_copy(part, part, l_recv.at[group, c]).wait()
        half = join([l_all[group, c, :, i].reshape(256, 128) for i in range(4)], operand[c], gather_s[...])
        t_tx[group, c] = jnp.where(first, half[:, 128:], half[:, :128])
        t_own[group, c] = jnp.where(first, half[:, :128], half[:, 128:])
        sibling_copy(group, c).start()

    def back(group, c):
        part = t_rx.at[group, c]
        pltpu.make_async_copy(part, part, t_recv.at[group, c]).wait()
        offset = off_s[pl.ds(pl.multiple_of((z * 2 + c) * 16, 16), 16), :]
        total = (t_own[group, c] + t_rx[group, c]).reshape(8, 16, 128) - offset[None]
        u_all[8 * group : 8 * group + 8, c] = total.astype(BF16)

        @pl.loop(8 * group, 8 * group + 8)
        def _(there):
            @pl.when(there == z)
            def _():
                pltpu.make_async_copy(u_all.at[there, c], f_rx.at[there, c], f_recv).start()

            @pl.when(there != z)
            def _():
                back_copy(c, there).start()

    left_out(0, 0)
    right_out(0)
    left_out(0, 1)
    right_out(1)
    left_out(1, 0)
    left_out(1, 1)
    product(0, 0)
    back(0, 0)
    product(0, 1)
    back(0, 1)
    product(1, 0)
    back(1, 0)
    product(1, 1)
    back(1, 1)

    pltpu.make_async_copy(f_rx, f_rx, f_recv).wait()
    values = finish(
        f_rx[...].reshape(512, 128), off_s[...], gain_s[...], bias_s[...], wide_s[...], out_b[...], roll
    )
    for q in range(4):
        update = values[q] * gate_s[q * 128 : (q + 1) * 128]
        out_ref[4 * q : 4 * q + 4] = update.astype(BF16).reshape(4, 32, 128)

    for c in range(2):
        for off in ORDER:
            edge_copy(0, c, off).wait_send()
            edge_copy(1, c, off).wait_send()
            back_copy(c, along_z(off)).wait_send()
        for group in range(2):
            sibling_copy(group, c).wait_send()
            for p in other_chips():
                left_copy(group, c, p).wait_send()
        for s in range(4):
            for hi in range(2):
                same, copy = right_copy(c, s, hi)

                @pl.when(jnp.logical_not(same))
                def _():
                    copy.wait_send()


def per_device(*args):
    args = [a.reshape(1, -1) if a.ndim == 1 else a for a in args]
    dma = pltpu.SemaphoreType.DMA
    return pl.pallas_call(
        kernel,
        out_shape=jax.ShapeDtypeStruct(args[0].shape, BF16),
        in_specs=[pl.BlockSpec(memory_space=pl.ANY)] * N_IN,
        out_specs=pl.BlockSpec(memory_space=pltpu.VMEM),
        scratch_shapes=[pltpu.VMEM(a.shape, a.dtype) for a in args]
        + [
            pltpu.VMEM((2, 2, 16, 16, 128), BF16),
            pltpu.VMEM((2, 2, 16, 16, 128), BF16),
            pltpu.VMEM((2, 2, 8, 4, 32, 128), BF16),
            pltpu.VMEM((2, 4, 2, 32, 128), BF16),
            pltpu.VMEM((2, 8, 2, 32, 128), BF16),
            pltpu.VMEM((2, 2, 128, 128), F32),
            pltpu.VMEM((2, 2, 128, 128), F32),
            pltpu.VMEM((2, 2, 128, 128), F32),
            pltpu.VMEM((16, 2, 16, 128), BF16),
            pltpu.VMEM((16, 2, 16, 128), BF16),
            pltpu.VMEM((512, 128), F32),
            pltpu.VMEM((1024, 256), BF16),
            pltpu.VMEM((512, 512), BF16),
            pltpu.VMEM((512, 128), F32),
            pltpu.VMEM((512, 128), F32),
            pltpu.VMEM((512, 128), F32),
            dma((N_IN,)), dma, dma((6,)), dma, dma((2, 2)), dma, dma((2,)), dma, dma((2, 2)), dma, dma,
        ],
        compiler_params=pltpu.CompilerParams(
            collective_id=0, has_side_effects=True, vmem_limit_bytes=56 * 1024 * 1024
        ),
    )(*args)


def solution(mesh):
    return jax.shard_map(
        per_device,
        mesh=mesh,
        in_specs=(P("row", "col", None), P(), P(), P(), P(), P(), P(), P(), P(), P(), P()),
        out_specs=P("row", "col", None),
        check_vma=False,
    )
```

```python
import jax
import jax.numpy as jnp
from jax import lax
from jax.experimental import pallas as pl
from jax.experimental.pallas import tpu as pltpu
from jax.sharding import PartitionSpec as P

MESH = pl.DeviceIdType.MESH
F32 = jnp.float32
BF16 = jnp.bfloat16


def dot_nn(a, b):
    return lax.dot_general(a, b, (((1,), (0,)), ((), ())), preferred_element_type=F32)


def dot_nt(a, b):
    return lax.dot_general(a, b, (((1,), (1,)), ((), ())), preferred_element_type=F32)


def iota(shape, dim):
    return lax.broadcasted_iota(jnp.int32, shape, dim)


def eye(n):
    return (iota((n, n), 0) == iota((n, n), 1)).astype(F32).astype(BF16)


def layer_norm_lanes(values, gain, bias):
    mean = jnp.mean(values, axis=-1, keepdims=True)
    centred = values - mean
    var = jnp.mean(centred * centred, axis=-1, keepdims=True)
    return centred * lax.rsqrt(var + 1e-05) * gain + bias


def sigmoid(x):
    return 1.0 / (1.0 + jnp.exp(-x))


def project(pair, gain, bias, proj_w, proj_b):
    normed = layer_norm_lanes(pair.astype(F32), gain, bias).astype(BF16)
    proj = dot_nn(normed, proj_w) + proj_b
    left = (sigmoid(proj[:, :128]) * proj[:, 128:256]).astype(BF16)
    right = (sigmoid(proj[:, 256:384]) * proj[:, 384:]).astype(BF16)
    return normed, left, right


def interleave(parts, roll):
    parts = [p.reshape(16, 8, p.shape[-1]) for p in parts]
    turned = [roll(p, 4, 1) for p in parts]
    low = iota(parts[0].shape, 1) < 4
    even = [jnp.where(low, parts[a], turned[a + 1]) for a in (0, 2)]
    odd = [jnp.where(low, turned[a], parts[a + 1]) for a in (0, 2)]
    return jnp.concatenate(even, axis=1), jnp.concatenate(odd, axis=1)


def edges_out(edge, roll):
    turned = dot_nt(eye(128), edge)
    even, odd = interleave([turned[:, q * 128 : (q + 1) * 128] for q in range(4)], roll)
    return even.astype(BF16), odd.astype(BF16)


def relay_left(rows):
    return dot_nt(eye(128), rows).astype(BF16).reshape(4, 32, 128)


def relay_right(rows):
    twice = jnp.concatenate([rows, rows], axis=0)
    r, c = iota((64, 128), 0), iota((64, 128), 1)
    base = (r // 32) * 64 + r % 32
    halves = [dot_nt(jnp.where(c == base + 32 * p, 1.0, 0.0).astype(BF16), twice) for p in range(2)]
    return jnp.where(c < 64, halves[0], halves[1]).astype(BF16).reshape(2, 32, 128)


def gather_const():
    a, b = iota((1024, 256), 0), iota((1024, 256), 1)
    i4, j4, core, zlo, q = a // 256, (a // 64) % 4, (a // 32) % 2, (a // 16) % 2, (a // 4) % 4
    goal = core * 128 + i4 * 32 + zlo * 16 + q * 4 + j4
    return jnp.where(goal == b, 1.0, 0.0).astype(BF16)


def join(left, right, gather):
    keep = iota((128, 256), 0) % 4 == iota((128, 256), 1) % 4
    high, low = [], []
    for block in left:
        both = lax.dot_general(block, right, (((0,), (0,)), ((), ())), preferred_element_type=F32)
        both = jnp.where(keep, both, 0.0)
        high.append(both.astype(BF16))
        low.append((both - high[-1].astype(F32)).astype(BF16))
    return dot_nn(jnp.concatenate(high, axis=1), gather) + dot_nn(jnp.concatenate(low, axis=1), gather)


def estimate(in_gain, in_bias, proj_w, proj_b):
    w = proj_w.astype(F32)

    def times(v, m):
        return dot_nn(jnp.concatenate([v] * 8, axis=0), m)[:1]

    mean = times(in_bias, w) + proj_b
    power = in_gain * in_gain
    total = 4.0 * 128.0
    for first in (0, 256):
        g, v = w[:, first : first + 128], w[:, first + 128 : first + 256]
        scale = lax.rsqrt(1.0 + (jnp.pi / 8) * times(power, g * g))
        gate = sigmoid(mean[:, first : first + 128] * scale)
        total = total * (
            gate * mean[:, first + 128 : first + 256] + times(power, g * v) * gate * (1.0 - gate) * scale
        )
    return total


def column(row):
    return jnp.transpose(jnp.broadcast_to(row, (128, 128)))


def group_sum(x, roll):
    row = iota(x.shape, 0)
    x = x + jnp.where(row % 2 == 0, roll(x, 15, 0), roll(x, 1, 0))
    return x + jnp.where(row % 4 < 2, roll(x, 14, 0), roll(x, 2, 0))


def spread(value, roll):
    even, odd = interleave([value] * 4, roll)
    return jnp.stack([even, odd], axis=1).reshape(512, value.shape[-1])


def wide_weight(out_w, roll):
    rows = spread(out_w.astype(F32), roll)
    q = (iota(rows.shape, 0) // 4) % 4
    return jnp.concatenate([jnp.where(q == p, rows, 0.0) for p in range(4)], axis=1).astype(BF16)


def finish(joined, offset, gain, bias, wide, out_b, roll):
    vals = (joined.astype(F32) + offset).reshape(32, 16, 128)
    mean = group_sum(jnp.sum(vals, axis=0), roll) * (1.0 / 128)
    centred = vals - mean[None]
    var = group_sum(jnp.sum(centred * centred, axis=0), roll) * (1.0 / 128)
    scale = lax.rsqrt(var + 1e-05)
    normed = (centred * scale[None]).reshape(512, 128) * gain + bias
    turned = dot_nt(eye(128), normed.astype(BF16)).astype(BF16)
    value = dot_nn(turned, wide)
    return [value[:, q * 128 : (q + 1) * 128] + out_b for q in range(4)]


N_IN = 11
ORDER = (8, 7, 9, 6, 10, 5, 11, 4, 12, 3, 13, 2, 14, 1, 15)


def kernel(*refs):
    hbm, out_ref, held, rest = refs[:N_IN], refs[N_IN], refs[N_IN + 1 : 2 * N_IN + 1], refs[2 * N_IN + 1 :]
    pair, in_gain, in_bias, proj_w, proj_b, norm_gain, norm_bias, out_w, out_b, gate_w, gate_b = held
    (
        x_tx, x_rx, l_all, r_tx, r_all, t_own, t_tx, t_rx, u_all, f_rx, gate_s, gather_s, wide_s, gain_s, bias_s, off_s,
        in_sem, x_send, x_recv, l_send, l_recv, r_send, r_recv, t_send, t_recv, f_send, f_recv,
    ) = rest
    roll = pltpu.roll
    row, col = lax.axis_index("row"), lax.axis_index("col")
    y_hi, z = lax.div(row, 16), lax.rem(row, 16)
    y_lo, x, core = lax.div(col, 8), lax.rem(lax.div(col, 2), 4), lax.rem(col, 2)
    chip = y_lo * 4 + x
    barrier = pltpu.get_barrier_semaphore()

    def along_z(off):
        return lax.rem(z + off, 16)

    def greet(device):
        pl.semaphore_signal(barrier, inc=1, device_id=device, device_id_type=MESH)

    for off in ORDER:
        greet((y_hi * 16 + along_z(off), col))
    fetch = [pltpu.make_async_copy(hbm[n], held[n], in_sem.at[n]) for n in range(N_IN)]
    for copy in fetch:
        copy.start()
    for t in range(1, 16):
        p = lax.rem(y_hi * 8 + chip + t, 16)
        greet((lax.div(p, 8) * 16 + z, lax.rem(p, 8) * 2 + core))
    sibling = (row, col + 1 - 2 * core)
    greet(sibling)

    for n in range(5):
        fetch[n].wait()
    normed, left, right = project(
        pair[...].reshape(512, 128), in_gain[...], in_bias[...], proj_w[...], proj_b[...]
    )
    for side, edge in enumerate((left, right)):
        even, odd = edges_out(edge, roll)
        x_tx[side, 0], x_tx[side, 1] = even, odd

    pl.semaphore_wait(barrier, 31)

    mine = lax.div(z, 8)

    def edge_semaphore(side, c):
        return x_recv.at[side * 4 + (1 - side) * 2 * mine + c]

    def edge_copy(side, c, off):
        there = along_z(off)
        return pltpu.make_async_remote_copy(
            src_ref=x_tx.at[side, c, there], dst_ref=x_rx.at[side, c, z], send_sem=x_send,
            recv_sem=edge_semaphore(side, c), device_id=(y_hi * 16 + there, col), device_id_type=MESH,
        )

    for turn in range(4):
        side = (1 - mine) * (0, 0, 1, 1)[turn] + mine * (1, 1, 0, 0)[turn]
        c = (1 - mine) * (0, 1, 0, 1)[turn] + mine * (0, 1, 0, 1)[turn]
        pltpu.make_async_copy(x_tx.at[side, c, z], x_rx.at[side, c, z], edge_semaphore(side, c)).start()
        for off in ORDER:
            edge_copy(side, c, off).start()

    for n in range(5, N_IN):
        fetch[n].wait()
    gate_s[...] = sigmoid(dot_nn(normed, gate_w[...]) + gate_b[...])
    off_s[...] = spread(column(estimate(in_gain[...], in_bias[...], proj_w[...], proj_b[...])), roll)
    wide_s[...] = wide_weight(out_w[...], roll)
    gain_s[...] = spread(column(norm_gain[...]), roll)
    bias_s[...] = spread(column(norm_bias[...]), roll)
    gather_s[...] = gather_const()

    def left_copy(group, c, p):
        return pltpu.make_async_remote_copy(
            src_ref=l_all.at[group, c, chip], dst_ref=l_all.at[group, c, chip], send_sem=l_send,
            recv_sem=l_recv.at[group, c], device_id=(row, p * 2 + core), device_id_type=MESH,
        )

    def other_chips():
        return [
            lax.rem(y_lo + dy, 2) * 4 + lax.rem(x + dx, 4)
            for dx, dy in ((2, 1), (2, 0), (1, 1), (3, 1), (1, 0), (3, 0), (0, 1))
        ]

    def left_out(group, c):
        part = x_rx.at[0, c, pl.ds(8 * group, 8)]
        pltpu.make_async_copy(part, part, x_recv.at[2 * group + c]).wait()
        l_all[group, c, chip] = relay_left(x_rx[0, c, 8 * group : 8 * group + 8].reshape(128, 128))
        for p in other_chips():
            left_copy(group, c, p).start()

    def right_copy(c, s, hi):
        there = (hi * 16 + z, y_hi * 8 + s * 2 + core)
        same = (there[0] == row) & (there[1] == col)
        return same, pltpu.make_async_remote_copy(
            src_ref=r_tx.at[c, s], dst_ref=r_all.at[c, chip], send_sem=r_send, recv_sem=r_recv.at[c],
            device_id=there, device_id_type=MESH,
        )

    def right_out(c):
        part = x_rx.at[1, c]
        pltpu.make_async_copy(part, part, x_recv.at[4 + c]).wait()
        for s in range(4):
            r_tx[c, s] = relay_right(x_rx[1, c, 4 * s : 4 * s + 4].reshape(64, 128))
        for s in range(4):
            for hi in range(2):
                same, copy = right_copy(c, s, hi)

                @pl.when(same)
                def _():
                    pltpu.make_async_copy(r_tx.at[c, s], r_all.at[c, chip], r_recv.at[c]).start()

                @pl.when(jnp.logical_not(same))
                def _():
                    copy.start()

    def sibling_copy(group, c):
        return pltpu.make_async_remote_copy(
            src_ref=t_tx.at[group, c], dst_ref=t_rx.at[group, c], send_sem=t_send, recv_sem=t_recv.at[group, c],
            device_id=sibling, device_id_type=MESH,
        )

    def back_copy(c, there):
        return pltpu.make_async_remote_copy(
            src_ref=u_all.at[there, c], dst_ref=f_rx.at[z, c], send_sem=f_send, recv_sem=f_recv,
            device_id=(y_hi * 16 + there, col), device_id_type=MESH,
        )

    first = core == 0
    operand = [None, None]

    def product(group, c):
        if operand[c] is None:
            part = r_all.at[c]
            pltpu.make_async_copy(part, part, r_recv.at[c]).wait()
            operand[c] = jnp.concatenate(
                [r_all[c, :, 0].reshape(256, 128), r_all[c, :, 1].reshape(256, 128)], axis=1
            )
        part = l_all.at[group, c, pl.ds(0, 7)]
        pltpu.make_async_copy(part, part, l_recv.at[group, c]).wait()
        half = join([l_all[group, c, :, i].reshape(256, 128) for i in range(4)], operand[c], gather_s[...])
        t_tx[group, c] = jnp.where(first, half[:, 128:], half[:, :128])
        t_own[group, c] = jnp.where(first, half[:, :128], half[:, 128:])
        sibling_copy(group, c).start()

    def back(group, c):
        part = t_rx.at[group, c]
        pltpu.make_async_copy(part, part, t_recv.at[group, c]).wait()
        offset = off_s[pl.ds(pl.multiple_of((z * 2 + c) * 16, 16), 16), :]
        total = (t_own[group, c] + t_rx[group, c]).reshape(8, 16, 128) - offset[None]
        u_all[8 * group : 8 * group + 8, c] = total.astype(BF16)

        @pl.loop(8 * group, 8 * group + 8)
        def _(there):
            @pl.when(there == z)
            def _():
                pltpu.make_async_copy(u_all.at[there, c], f_rx.at[there, c], f_recv).start()

            @pl.when(there != z)
            def _():
                back_copy(c, there).start()

    left_out(0, 0)
    left_out(0, 1)
    right_out(0)
    right_out(1)
    left_out(1, 0)
    left_out(1, 1)
    product(0, 0)
    back(0, 0)
    product(0, 1)
    back(0, 1)
    product(1, 0)
    back(1, 0)
    product(1, 1)
    back(1, 1)

    def left_here(part, semaphore):
        pltpu.make_async_copy(part, part, semaphore).wait()

    left_here(x_tx.at[:, :, pl.ds(0, 15)], x_send)
    left_here(l_all.at[:, :, pl.ds(0, 7)], l_send)
    left_here(r_all.at[:, pl.ds(0, 7)], r_send)

    @pl.when(y_lo != y_hi)
    def _():
        left_here(r_all.at[:, pl.ds(0, 1)], r_send)

    left_here(t_tx, t_send)
    left_here(f_rx.at[pl.ds(0, 15)], f_send)

    pltpu.make_async_copy(f_rx, f_rx, f_recv).wait()
    values = finish(
        f_rx[...].reshape(512, 128), off_s[...], gain_s[...], bias_s[...], wide_s[...], out_b[...], roll
    )
    for q in range(4):
        update = values[q] * gate_s[q * 128 : (q + 1) * 128]
        out_ref[4 * q : 4 * q + 4] = update.astype(BF16).reshape(4, 32, 128)


def per_device(*args):
    args = [a.reshape(1, -1) if a.ndim == 1 else a for a in args]
    dma = pltpu.SemaphoreType.DMA
    return pl.pallas_call(
        kernel,
        out_shape=jax.ShapeDtypeStruct(args[0].shape, BF16),
        in_specs=[pl.BlockSpec(memory_space=pl.ANY)] * N_IN,
        out_specs=pl.BlockSpec(memory_space=pltpu.VMEM),
        scratch_shapes=[pltpu.VMEM(a.shape, a.dtype) for a in args]
        + [
            pltpu.VMEM((2, 2, 16, 16, 128), BF16),
            pltpu.VMEM((2, 2, 16, 16, 128), BF16),
            pltpu.VMEM((2, 2, 8, 4, 32, 128), BF16),
            pltpu.VMEM((2, 4, 2, 32, 128), BF16),
            pltpu.VMEM((2, 8, 2, 32, 128), BF16),
            pltpu.VMEM((2, 2, 128, 128), F32),
            pltpu.VMEM((2, 2, 128, 128), F32),
            pltpu.VMEM((2, 2, 128, 128), F32),
            pltpu.VMEM((16, 2, 16, 128), BF16),
            pltpu.VMEM((16, 2, 16, 128), BF16),
            pltpu.VMEM((512, 128), F32),
            pltpu.VMEM((1024, 256), BF16),
            pltpu.VMEM((512, 512), BF16),
            pltpu.VMEM((512, 128), F32),
            pltpu.VMEM((512, 128), F32),
            pltpu.VMEM((512, 128), F32),
            dma((N_IN,)), dma, dma((6,)), dma, dma((2, 2)), dma, dma((2,)), dma, dma((2, 2)), dma, dma,
        ],
        compiler_params=pltpu.CompilerParams(
            collective_id=0, has_side_effects=True, vmem_limit_bytes=40 * 1024 * 1024
        ),
    )(*[pltpu.with_memory_space_constraint(a, pltpu.HBM) for a in args])


def solution(mesh):
    return jax.shard_map(
        per_device,
        mesh=mesh,
        in_specs=(P("row", "col", None), P(), P(), P(), P(), P(), P(), P(), P(), P(), P()),
        out_specs=P("row", "col", None),
        check_vma=False,
    )
```

```python
import jax
import jax.numpy as jnp
from jax import lax
from jax.experimental import pallas as pl
from jax.experimental.pallas import tpu as pltpu
from jax.sharding import PartitionSpec as P

MESH = pl.DeviceIdType.MESH
F32 = jnp.float32
BF16 = jnp.bfloat16


def dot_nn(a, b):
    return lax.dot_general(a, b, (((1,), (0,)), ((), ())), preferred_element_type=F32)


def dot_nt(a, b):
    return lax.dot_general(a, b, (((1,), (1,)), ((), ())), preferred_element_type=F32)


def iota(shape, dim):
    return lax.broadcasted_iota(jnp.int32, shape, dim)


def eye(n):
    return (iota((n, n), 0) == iota((n, n), 1)).astype(F32).astype(BF16)


def layer_norm_lanes(values, gain, bias):
    mean = jnp.mean(values, axis=-1, keepdims=True)
    centred = values - mean
    var = jnp.mean(centred * centred, axis=-1, keepdims=True)
    return centred * lax.rsqrt(var + 1e-05) * gain + bias


def sigmoid(x):
    return 1.0 / (1.0 + jnp.exp(-x))


def project(pair, gain, bias, proj_w, proj_b):
    normed = layer_norm_lanes(pair.astype(F32), gain, bias).astype(BF16)
    proj = dot_nn(normed, proj_w) + proj_b
    left = (sigmoid(proj[:, :128]) * proj[:, 128:256]).astype(BF16)
    right = (sigmoid(proj[:, 256:384]) * proj[:, 384:]).astype(BF16)
    return normed, left, right


def interleave(parts, roll):
    parts = [p.reshape(16, 8, p.shape[-1]) for p in parts]
    turned = [roll(p, 4, 1) for p in parts]
    low = iota(parts[0].shape, 1) < 4
    even = [jnp.where(low, parts[a], turned[a + 1]) for a in (0, 2)]
    odd = [jnp.where(low, turned[a], parts[a + 1]) for a in (0, 2)]
    return jnp.concatenate(even, axis=1), jnp.concatenate(odd, axis=1)


def edges_out(edge, roll):
    turned = dot_nt(eye(128), edge)
    even, odd = interleave([turned[:, q * 128 : (q + 1) * 128] for q in range(4)], roll)
    return even.astype(BF16), odd.astype(BF16)


def relay_left(rows):
    return dot_nt(eye(128), rows).astype(BF16).reshape(4, 32, 128)


def relay_right(rows):
    turned = dot_nt(eye(128), rows)
    low = iota((32, 128), 1) < 64
    out = []
    for s in range(4):
        pair = turned[:, 128 * (s // 2) : 128 * (s // 2) + 128].reshape(4, 32, 128)
        swapped = [pltpu.roll(pair[j], 64, 1) for j in range(4)]
        first, second = (pair, swapped) if s % 2 == 0 else (swapped, pair)
        out.append([jnp.where(low, first[2 * t], second[2 * t + 1]).astype(BF16) for t in range(2)])
    return out


def gather_const():
    a, b = iota((1024, 256), 0), iota((1024, 256), 1)
    i4, j4, core, zlo, q = a // 256, (a // 64) % 4, (a // 32) % 2, (a // 16) % 2, (a // 4) % 4
    goal = core * 128 + i4 * 32 + zlo * 16 + q * 4 + j4
    return jnp.where(goal == b, 1.0, 0.0).astype(BF16)


def join(left, right, gather):
    keep = iota((128, 256), 0) % 4 == iota((128, 256), 1) % 4
    high, low = [], []
    for block in left:
        both = lax.dot_general(block, right, (((0,), (0,)), ((), ())), preferred_element_type=F32)
        both = jnp.where(keep, both, 0.0)
        high.append(both.astype(BF16))
        low.append((both - high[-1].astype(F32)).astype(BF16))
    return dot_nn(jnp.concatenate(high, axis=1), gather) + dot_nn(jnp.concatenate(low, axis=1), gather)


def estimate(in_gain, in_bias, proj_w, proj_b):
    w = proj_w.astype(F32)

    def times(v, m):
        return dot_nn(jnp.concatenate([v] * 8, axis=0), m)[:1]

    mean = times(in_bias, w) + proj_b
    power = in_gain * in_gain
    total = 4.0 * 128.0
    for first in (0, 256):
        g, v = w[:, first : first + 128], w[:, first + 128 : first + 256]
        scale = lax.rsqrt(1.0 + (jnp.pi / 8) * times(power, g * g))
        gate = sigmoid(mean[:, first : first + 128] * scale)
        total = total * (
            gate * mean[:, first + 128 : first + 256] + times(power, g * v) * gate * (1.0 - gate) * scale
        )
    return total


def column(row):
    return jnp.transpose(jnp.broadcast_to(row, (128, 128)))


def group_sum(x, roll):
    row = iota(x.shape, 0)
    x = x + jnp.where(row % 2 == 0, roll(x, 15, 0), roll(x, 1, 0))
    return x + jnp.where(row % 4 < 2, roll(x, 14, 0), roll(x, 2, 0))


def spread(value, roll):
    even, odd = interleave([value] * 4, roll)
    return jnp.stack([even, odd], axis=1).reshape(512, value.shape[-1])


def wide_weight(out_w, roll):
    rows = spread(out_w.astype(F32), roll)
    q = (iota(rows.shape, 0) // 4) % 4
    return jnp.concatenate([jnp.where(q == p, rows, 0.0) for p in range(4)], axis=1).astype(BF16)


def finish(joined, offset, gain, bias, wide, out_b, roll):
    vals = (joined.astype(F32) + offset).reshape(32, 16, 128)
    mean = group_sum(jnp.sum(vals, axis=0), roll) * (1.0 / 128)
    centred = vals - mean[None]
    var = group_sum(jnp.sum(centred * centred, axis=0), roll) * (1.0 / 128)
    scale = lax.rsqrt(var + 1e-05)
    normed = (centred * scale[None]).reshape(512, 128) * gain + bias
    value = lax.dot_general(normed.astype(BF16), wide, (((0,), (0,)), ((), ())), preferred_element_type=F32)
    return [value[:, q * 128 : (q + 1) * 128] + out_b for q in range(4)]


N_IN = 11
ORDER = (8, 7, 9, 6, 10, 5, 11, 4, 12, 3, 13, 2, 14, 1, 15)


def kernel(*refs):
    hbm, out_ref, held, rest = refs[:N_IN], refs[N_IN], refs[N_IN + 1 : 2 * N_IN + 1], refs[2 * N_IN + 1 :]
    pair, in_gain, in_bias, proj_w, proj_b, norm_gain, norm_bias, out_w, out_b, gate_w, gate_b = held
    (
        x_tx, x_rx, l_all, r_tx, r_all, t_own, t_tx, t_rx, u_all, f_rx, gate_s, gather_s, wide_s, gain_s, bias_s, off_s,
        in_sem, x_send, x_recv, l_send, l_recv, r_send, r_recv, t_send, t_recv, f_send, f_recv,
    ) = rest
    roll = pltpu.roll
    row, col = lax.axis_index("row"), lax.axis_index("col")
    y_hi, z = lax.div(row, 16), lax.rem(row, 16)
    y_lo, x, core = lax.div(col, 8), lax.rem(lax.div(col, 2), 4), lax.rem(col, 2)
    chip = y_lo * 4 + x
    barrier = pltpu.get_barrier_semaphore()

    def along_z(off):
        return lax.rem(z + off, 16)

    def greet(device):
        pl.semaphore_signal(barrier, inc=1, device_id=device, device_id_type=MESH)

    for off in ORDER:
        greet((y_hi * 16 + along_z(off), col))
    fetch = [pltpu.make_async_copy(hbm[n], held[n], in_sem.at[n]) for n in range(N_IN)]
    for copy in fetch:
        copy.start()
    for t in range(1, 16):
        p = lax.rem(y_hi * 8 + chip + t, 16)
        greet((lax.div(p, 8) * 16 + z, lax.rem(p, 8) * 2 + core))
    sibling = (row, col + 1 - 2 * core)
    greet(sibling)

    for n in range(5):
        fetch[n].wait()
    normed, left, right = project(
        pair[...].reshape(512, 128), in_gain[...], in_bias[...], proj_w[...], proj_b[...]
    )
    for side, edge in enumerate((left, right)):
        even, odd = edges_out(edge, roll)
        x_tx[side, 0], x_tx[side, 1] = even, odd

    pl.semaphore_wait(barrier, 31)

    mine = lax.div(z, 8)

    def edge_semaphore(side, c):
        return x_recv.at[side * 4 + (1 - side) * 2 * mine + c]

    def edge_copy(side, c, off):
        there = along_z(off)
        return pltpu.make_async_remote_copy(
            src_ref=x_tx.at[side, c, there], dst_ref=x_rx.at[side, c, z], send_sem=x_send,
            recv_sem=edge_semaphore(side, c), device_id=(y_hi * 16 + there, col), device_id_type=MESH,
        )

    for turn in range(4):
        side = (1 - mine) * (0, 0, 1, 1)[turn] + mine * (1, 0, 1, 0)[turn]
        c = (1 - mine) * (0, 1, 0, 1)[turn] + mine * (0, 0, 1, 1)[turn]
        pltpu.make_async_copy(x_tx.at[side, c, z], x_rx.at[side, c, z], edge_semaphore(side, c)).start()
        for off in ORDER:
            edge_copy(side, c, off).start()

    for n in range(5, N_IN):
        fetch[n].wait()
    gate_s[...] = sigmoid(dot_nn(normed, gate_w[...]) + gate_b[...])
    off_s[...] = spread(column(estimate(in_gain[...], in_bias[...], proj_w[...], proj_b[...])), roll)
    wide_s[...] = wide_weight(out_w[...], roll)
    gain_s[...] = spread(column(norm_gain[...]), roll)
    bias_s[...] = spread(column(norm_bias[...]), roll)
    gather_s[...] = gather_const()

    def left_copy(group, c, p):
        return pltpu.make_async_remote_copy(
            src_ref=l_all.at[group, c, chip], dst_ref=l_all.at[group, c, chip], send_sem=l_send,
            recv_sem=l_recv.at[group, c], device_id=(row, p * 2 + core), device_id_type=MESH,
        )

    def other_chips():
        return [
            lax.rem(y_lo + dy, 2) * 4 + lax.rem(x + dx, 4)
            for dx, dy in ((2, 1), (2, 0), (1, 1), (3, 1), (1, 0), (3, 0), (0, 1))
        ]

    def left_out(group, c):
        part = x_rx.at[0, c, pl.ds(8 * group, 8)]
        pltpu.make_async_copy(part, part, x_recv.at[2 * group + c]).wait()
        l_all[group, c, chip] = relay_left(x_rx[0, c, 8 * group : 8 * group + 8].reshape(128, 128))
        for p in other_chips():
            left_copy(group, c, p).start()

    def right_copy(c, s, hi):
        there = (hi * 16 + z, y_hi * 8 + s * 2 + core)
        same = (there[0] == row) & (there[1] == col)
        return same, pltpu.make_async_remote_copy(
            src_ref=r_tx.at[c, s], dst_ref=r_all.at[c, chip], send_sem=r_send, recv_sem=r_recv.at[c],
            device_id=there, device_id_type=MESH,
        )

    def right_out(c):
        part = x_rx.at[1, c]
        pltpu.make_async_copy(part, part, x_recv.at[4 + c]).wait()
        blocks = relay_right(x_rx[1, c].reshape(256, 128))
        for s in range(4):
            r_tx[c, s, 0], r_tx[c, s, 1] = blocks[s]
        for s in range(4):
            for hi in range(2):
                same, copy = right_copy(c, s, hi)

                @pl.when(same)
                def _():
                    pltpu.make_async_copy(r_tx.at[c, s], r_all.at[c, chip], r_recv.at[c]).start()

                @pl.when(jnp.logical_not(same))
                def _():
                    copy.start()

    def sibling_copy(group, c):
        return pltpu.make_async_remote_copy(
            src_ref=t_tx.at[group, c], dst_ref=t_rx.at[group, c], send_sem=t_send, recv_sem=t_recv.at[group, c],
            device_id=sibling, device_id_type=MESH,
        )

    def back_copy(c, there):
        return pltpu.make_async_remote_copy(
            src_ref=u_all.at[there, c], dst_ref=f_rx.at[z, c], send_sem=f_send, recv_sem=f_recv,
            device_id=(y_hi * 16 + there, col), device_id_type=MESH,
        )

    first = core == 0
    operand = [None, None]

    def product(group, c):
        if operand[c] is None:
            part = r_all.at[c]
            pltpu.make_async_copy(part, part, r_recv.at[c]).wait()
            operand[c] = jnp.concatenate(
                [r_all[c, :, 0].reshape(256, 128), r_all[c, :, 1].reshape(256, 128)], axis=1
            )
        part = l_all.at[group, c, pl.ds(0, 7)]
        pltpu.make_async_copy(part, part, l_recv.at[group, c]).wait()
        half = join([l_all[group, c, :, i].reshape(256, 128) for i in range(4)], operand[c], gather_s[...])
        t_tx[group, c] = jnp.where(first, half[:, 128:], half[:, :128])
        t_own[group, c] = jnp.where(first, half[:, :128], half[:, 128:])
        sibling_copy(group, c).start()

    def back(group, c):
        part = t_rx.at[group, c]
        pltpu.make_async_copy(part, part, t_recv.at[group, c]).wait()
        offset = off_s[pl.ds(pl.multiple_of((z * 2 + c) * 16, 16), 16), :]
        total = (t_own[group, c] + t_rx[group, c]).reshape(8, 16, 128) - offset[None]
        u_all[8 * group : 8 * group + 8, c] = total.astype(BF16)

        @pl.loop(8 * group, 8 * group + 8)
        def _(there):
            @pl.when(there == z)
            def _():
                pltpu.make_async_copy(u_all.at[there, c], f_rx.at[there, c], f_recv).start()

            @pl.when(there != z)
            def _():
                back_copy(c, there).start()

    left_out(0, 0)
    left_out(0, 1)
    right_out(0)
    right_out(1)
    left_out(1, 0)
    left_out(1, 1)
    product(0, 0)
    back(0, 0)
    product(0, 1)
    back(0, 1)
    product(1, 0)
    back(1, 0)
    product(1, 1)
    back(1, 1)

    def left_here(part, semaphore):
        pltpu.make_async_copy(part, part, semaphore).wait()

    left_here(x_tx.at[:, :, pl.ds(0, 15)], x_send)
    left_here(l_all.at[:, :, pl.ds(0, 7)], l_send)
    left_here(r_all.at[:, pl.ds(0, 7)], r_send)

    @pl.when(y_lo != y_hi)
    def _():
        left_here(r_all.at[:, pl.ds(0, 1)], r_send)

    left_here(t_tx, t_send)
    left_here(f_rx.at[pl.ds(0, 15)], f_send)

    pltpu.make_async_copy(f_rx, f_rx, f_recv).wait()
    values = finish(
        f_rx[...].reshape(512, 128), off_s[...], gain_s[...], bias_s[...], wide_s[...], out_b[...], roll
    )
    for q in range(4):
        update = values[q] * gate_s[q * 128 : (q + 1) * 128]
        out_ref[4 * q : 4 * q + 4] = update.astype(BF16).reshape(4, 32, 128)


def per_device(*args):
    args = [a.reshape(1, -1) if a.ndim == 1 else a for a in args]
    dma = pltpu.SemaphoreType.DMA
    return pl.pallas_call(
        kernel,
        out_shape=jax.ShapeDtypeStruct(args[0].shape, BF16),
        in_specs=[pl.BlockSpec(memory_space=pl.ANY)] * N_IN,
        out_specs=pl.BlockSpec(memory_space=pltpu.VMEM),
        scratch_shapes=[pltpu.VMEM(a.shape, a.dtype) for a in args]
        + [
            pltpu.VMEM((2, 2, 16, 16, 128), BF16),
            pltpu.VMEM((2, 2, 16, 16, 128), BF16),
            pltpu.VMEM((2, 2, 8, 4, 32, 128), BF16),
            pltpu.VMEM((2, 4, 2, 32, 128), BF16),
            pltpu.VMEM((2, 8, 2, 32, 128), BF16),
            pltpu.VMEM((2, 2, 128, 128), F32),
            pltpu.VMEM((2, 2, 128, 128), F32),
            pltpu.VMEM((2, 2, 128, 128), F32),
            pltpu.VMEM((16, 2, 16, 128), BF16),
            pltpu.VMEM((16, 2, 16, 128), BF16),
            pltpu.VMEM((512, 128), F32),
            pltpu.VMEM((1024, 256), BF16),
            pltpu.VMEM((512, 512), BF16),
            pltpu.VMEM((512, 128), F32),
            pltpu.VMEM((512, 128), F32),
            pltpu.VMEM((512, 128), F32),
            dma((N_IN,)), dma, dma((6,)), dma, dma((2, 2)), dma, dma((2,)), dma, dma((2, 2)), dma, dma,
        ],
        compiler_params=pltpu.CompilerParams(
            collective_id=0, has_side_effects=True, vmem_limit_bytes=40 * 1024 * 1024
        ),
    )(*[pltpu.with_memory_space_constraint(a, pltpu.HBM) for a in args])


def solution(mesh):
    return jax.shard_map(
        per_device,
        mesh=mesh,
        in_specs=(P("row", "col", None), P(), P(), P(), P(), P(), P(), P(), P(), P(), P()),
        out_specs=P("row", "col", None),
        check_vma=False,
    )
```

```python
import jax
import jax.numpy as jnp
from jax import lax
from jax.experimental import pallas as pl
from jax.experimental.pallas import tpu as pltpu
from jax.sharding import PartitionSpec as P

MESH = pl.DeviceIdType.MESH
F32 = jnp.float32
BF16 = jnp.bfloat16


def dot_nn(a, b):
    return lax.dot_general(a, b, (((1,), (0,)), ((), ())), preferred_element_type=F32)


def dot_nt(a, b):
    return lax.dot_general(a, b, (((1,), (1,)), ((), ())), preferred_element_type=F32)


def iota(shape, dim):
    return lax.broadcasted_iota(jnp.int32, shape, dim)


def eye(n):
    return (iota((n, n), 0) == iota((n, n), 1)).astype(F32).astype(BF16)


def layer_norm_lanes(values, gain, bias):
    mean = jnp.mean(values, axis=-1, keepdims=True)
    centred = values - mean
    var = jnp.mean(centred * centred, axis=-1, keepdims=True)
    return centred * lax.rsqrt(var + 1e-05) * gain + bias


def sigmoid(x):
    return 1.0 / (1.0 + jnp.exp(-x))


def project(pair, gain, bias, proj_w, proj_b):
    normed = layer_norm_lanes(pair.astype(F32), gain, bias).astype(BF16)
    proj = dot_nn(normed, proj_w) + proj_b
    left = (sigmoid(proj[:, :128]) * proj[:, 128:256]).astype(BF16)
    right = (sigmoid(proj[:, 256:384]) * proj[:, 384:]).astype(BF16)
    return normed, left, right


def interleave(parts, roll):
    parts = [p.reshape(16, 8, p.shape[-1]) for p in parts]
    turned = [roll(p, 4, 1) for p in parts]
    low = iota(parts[0].shape, 1) < 4
    even = [jnp.where(low, parts[a], turned[a + 1]) for a in (0, 2)]
    odd = [jnp.where(low, turned[a], parts[a + 1]) for a in (0, 2)]
    return jnp.concatenate(even, axis=1), jnp.concatenate(odd, axis=1)


def edges_out(edge, roll):
    turned = dot_nt(eye(128), edge)
    even, odd = interleave([turned[:, q * 128 : (q + 1) * 128] for q in range(4)], roll)
    return even.astype(BF16), odd.astype(BF16)


def relay_left(rows):
    return dot_nt(eye(128), rows).astype(BF16).reshape(4, 32, 128)


def relay_right(rows):
    turned = dot_nt(eye(128), rows)
    low = iota((32, 128), 1) < 64
    out = []
    for s in range(4):
        pair = turned[:, 128 * (s // 2) : 128 * (s // 2) + 128].reshape(4, 32, 128)
        swapped = [pltpu.roll(pair[j], 64, 1) for j in range(4)]
        first, second = (pair, swapped) if s % 2 == 0 else (swapped, pair)
        out.append([jnp.where(low, first[2 * t], second[2 * t + 1]).astype(BF16) for t in range(2)])
    return out


def gather_const():
    a, b = iota((1024, 256), 0), iota((1024, 256), 1)
    i4, j4, core, zlo, q = a // 256, (a // 64) % 4, (a // 32) % 2, (a // 16) % 2, (a // 4) % 4
    goal = core * 128 + i4 * 32 + zlo * 16 + q * 4 + j4
    return jnp.where(goal == b, 1.0, 0.0).astype(BF16)


def join(left, right, gather):
    keep = iota((128, 256), 0) % 4 == iota((128, 256), 1) % 4
    high, low = [], []
    for block in left:
        both = lax.dot_general(block, right, (((0,), (0,)), ((), ())), preferred_element_type=F32)
        both = jnp.where(keep, both, 0.0)
        high.append(both.astype(BF16))
        low.append((both - high[-1].astype(F32)).astype(BF16))
    return dot_nn(jnp.concatenate(high, axis=1), gather) + dot_nn(jnp.concatenate(low, axis=1), gather)


def estimate(in_gain, in_bias, proj_w, proj_b):
    w = proj_w.astype(F32)

    def times(v, m):
        return dot_nn(jnp.concatenate([v] * 8, axis=0), m)[:1]

    mean = times(in_bias, w) + proj_b
    power = in_gain * in_gain
    total = 4.0 * 128.0
    for first in (0, 256):
        g, v = w[:, first : first + 128], w[:, first + 128 : first + 256]
        scale = lax.rsqrt(1.0 + (jnp.pi / 8) * times(power, g * g))
        gate = sigmoid(mean[:, first : first + 128] * scale)
        total = total * (
            gate * mean[:, first + 128 : first + 256] + times(power, g * v) * gate * (1.0 - gate) * scale
        )
    return total


def column(row):
    return jnp.transpose(jnp.broadcast_to(row, (128, 128)))


def group_sum(x, roll):
    row = iota(x.shape, 0)
    x = x + jnp.where(row % 2 == 0, roll(x, 15, 0), roll(x, 1, 0))
    return x + jnp.where(row % 4 < 2, roll(x, 14, 0), roll(x, 2, 0))


def spread(value, roll):
    even, odd = interleave([value] * 4, roll)
    return jnp.stack([even, odd], axis=1).reshape(512, value.shape[-1])


def wide_weight(out_w, roll):
    rows = spread(out_w.astype(F32), roll)
    q = (iota(rows.shape, 0) // 4) % 4
    return jnp.concatenate([jnp.where(q == p, rows, 0.0) for p in range(4)], axis=1).astype(BF16)


def finish(joined, offset, gain, bias, wide, out_b, roll):
    vals = (joined.astype(F32) + offset).reshape(32, 16, 128)
    mean = group_sum(jnp.sum(vals, axis=0), roll) * (1.0 / 128)
    centred = vals - mean[None]
    var = group_sum(jnp.sum(centred * centred, axis=0), roll) * (1.0 / 128)
    scale = lax.rsqrt(var + 1e-05)
    normed = (centred * scale[None]).reshape(512, 128) * gain + bias
    value = lax.dot_general(normed.astype(BF16), wide, (((0,), (0,)), ((), ())), preferred_element_type=F32)
    return [value[:, q * 128 : (q + 1) * 128] + out_b for q in range(4)]


N_IN = 11
ORDER = (8, 7, 9, 6, 10, 5, 11, 4, 12, 3, 13, 2, 14, 1, 15)


def kernel(*refs):
    hbm, out_ref, held, rest = refs[:N_IN], refs[N_IN], refs[N_IN + 1 : 2 * N_IN + 1], refs[2 * N_IN + 1 :]
    pair, in_gain, in_bias, proj_w, proj_b, norm_gain, norm_bias, out_w, out_b, gate_w, gate_b = held
    (
        x_tx, x_rx, l_all, r_tx, r_all, t_own, t_tx, t_rx, u_all, f_rx, gate_s, gather_s, wide_s, gain_s, bias_s, off_s,
        in_sem, x_send, x_recv, l_send, l_recv, r_send, r_recv, t_send, t_recv, f_send, f_recv,
    ) = rest
    roll = pltpu.roll
    row, col = lax.axis_index("row"), lax.axis_index("col")
    y_hi, z = lax.div(row, 16), lax.rem(row, 16)
    y_lo, x, core = lax.div(col, 8), lax.rem(lax.div(col, 2), 4), lax.rem(col, 2)
    chip = y_lo * 4 + x
    barrier = pltpu.get_barrier_semaphore()

    def along_z(off):
        return lax.rem(z + off, 16)

    def greet(device):
        pl.semaphore_signal(barrier, inc=1, device_id=device, device_id_type=MESH)

    for off in ORDER:
        greet((y_hi * 16 + along_z(off), col))
    fetch = [pltpu.make_async_copy(hbm[n], held[n], in_sem.at[n]) for n in range(N_IN)]
    for copy in fetch:
        copy.start()
    for t in range(1, 8):
        greet((row, lax.rem(chip + t, 8) * 2 + core))

    @pl.when(y_lo != y_hi)
    def _():
        for p in range(8):
            greet(((1 - y_hi) * 16 + z, p * 2 + core))

    sibling = (row, col + 1 - 2 * core)
    greet(sibling)

    for n in range(5):
        fetch[n].wait()
    normed, left, right = project(
        pair[...].reshape(512, 128), in_gain[...], in_bias[...], proj_w[...], proj_b[...]
    )
    for side, edge in enumerate((left, right)):
        even, odd = edges_out(edge, roll)
        x_tx[side, 0], x_tx[side, 1] = even, odd

    pl.semaphore_wait(barrier, 27)

    mine = lax.div(z, 8)

    def edge_semaphore(side, c):
        return x_recv.at[side * 4 + (1 - side) * 2 * mine + c]

    def edge_copy(side, c, off):
        there = along_z(off)
        return pltpu.make_async_remote_copy(
            src_ref=x_tx.at[side, c, there], dst_ref=x_rx.at[side, c, z], send_sem=x_send,
            recv_sem=edge_semaphore(side, c), device_id=(y_hi * 16 + there, col), device_id_type=MESH,
        )

    for turn in range(4):
        side = (1 - mine) * (0, 0, 1, 1)[turn] + mine * (1, 0, 1, 0)[turn]
        c = (1 - mine) * (0, 1, 0, 1)[turn] + mine * (0, 0, 1, 1)[turn]
        pltpu.make_async_copy(x_tx.at[side, c, z], x_rx.at[side, c, z], edge_semaphore(side, c)).start()
        for off in ORDER:
            edge_copy(side, c, off).start()

    for n in range(5, N_IN):
        fetch[n].wait()
    gate_s[...] = sigmoid(dot_nn(normed, gate_w[...]) + gate_b[...])
    off_s[...] = spread(column(estimate(in_gain[...], in_bias[...], proj_w[...], proj_b[...])), roll)
    wide_s[...] = wide_weight(out_w[...], roll)
    gain_s[...] = spread(column(norm_gain[...]), roll)
    bias_s[...] = spread(column(norm_bias[...]), roll)
    gather_s[...] = gather_const()

    def left_copy(group, c, p):
        return pltpu.make_async_remote_copy(
            src_ref=l_all.at[group, c, chip], dst_ref=l_all.at[group, c, chip], send_sem=l_send,
            recv_sem=l_recv.at[group, c], device_id=(row, p * 2 + core), device_id_type=MESH,
        )

    def other_chips():
        return [
            lax.rem(y_lo + dy, 2) * 4 + lax.rem(x + dx, 4)
            for dx, dy in ((2, 1), (2, 0), (1, 1), (3, 1), (1, 0), (3, 0), (0, 1))
        ]

    def left_out(group, c):
        part = x_rx.at[0, c, pl.ds(8 * group, 8)]
        pltpu.make_async_copy(part, part, x_recv.at[2 * group + c]).wait()
        l_all[group, c, chip] = relay_left(x_rx[0, c, 8 * group : 8 * group + 8].reshape(128, 128))
        for p in other_chips():
            left_copy(group, c, p).start()

    def right_copy(c, s, hi):
        there = (hi * 16 + z, y_hi * 8 + s * 2 + core)
        same = (there[0] == row) & (there[1] == col)
        return same, pltpu.make_async_remote_copy(
            src_ref=r_tx.at[c, s], dst_ref=r_all.at[c, chip], send_sem=r_send, recv_sem=r_recv.at[c],
            device_id=there, device_id_type=MESH,
        )

    def right_out(c):
        part = x_rx.at[1, c]
        pltpu.make_async_copy(part, part, x_recv.at[4 + c]).wait()
        blocks = relay_right(x_rx[1, c].reshape(256, 128))
        for s in range(4):
            r_tx[c, s, 0], r_tx[c, s, 1] = blocks[s]
        for s in range(4):
            for hi in range(2):
                same, copy = right_copy(c, s, hi)

                @pl.when(same)
                def _():
                    pltpu.make_async_copy(r_tx.at[c, s], r_all.at[c, chip], r_recv.at[c]).start()

                @pl.when(jnp.logical_not(same))
                def _():
                    copy.start()

    def sibling_copy(group, c):
        return pltpu.make_async_remote_copy(
            src_ref=t_tx.at[group, c], dst_ref=t_rx.at[group, c], send_sem=t_send, recv_sem=t_recv.at[group, c],
            device_id=sibling, device_id_type=MESH,
        )

    def back_copy(c, there):
        return pltpu.make_async_remote_copy(
            src_ref=u_all.at[there, c], dst_ref=f_rx.at[z, c], send_sem=f_send, recv_sem=f_recv,
            device_id=(y_hi * 16 + there, col), device_id_type=MESH,
        )

    first = core == 0
    operand = [None, None]

    def product(group, c):
        if operand[c] is None:
            part = r_all.at[c]
            pltpu.make_async_copy(part, part, r_recv.at[c]).wait()
            operand[c] = jnp.concatenate(
                [r_all[c, :, 0].reshape(256, 128), r_all[c, :, 1].reshape(256, 128)], axis=1
            )
        part = l_all.at[group, c, pl.ds(0, 7)]
        pltpu.make_async_copy(part, part, l_recv.at[group, c]).wait()
        half = join([l_all[group, c, :, i].reshape(256, 128) for i in range(4)], operand[c], gather_s[...])
        t_tx[group, c] = jnp.where(first, half[:, 128:], half[:, :128])
        t_own[group, c] = jnp.where(first, half[:, :128], half[:, 128:])
        sibling_copy(group, c).start()

    def back(group, c):
        part = t_rx.at[group, c]
        pltpu.make_async_copy(part, part, t_recv.at[group, c]).wait()
        offset = off_s[pl.ds(pl.multiple_of((z * 2 + c) * 16, 16), 16), :]
        total = (t_own[group, c] + t_rx[group, c]).reshape(8, 16, 128) - offset[None]
        u_all[8 * group : 8 * group + 8, c] = total.astype(BF16)

        @pl.loop(8 * group, 8 * group + 8)
        def _(there):
            @pl.when(there == z)
            def _():
                pltpu.make_async_copy(u_all.at[there, c], f_rx.at[there, c], f_recv).start()

            @pl.when(there != z)
            def _():
                back_copy(c, there).start()

    left_out(0, 0)
    left_out(0, 1)
    right_out(0)
    right_out(1)
    left_out(1, 0)
    left_out(1, 1)
    product(0, 0)
    back(0, 0)
    product(0, 1)
    back(0, 1)
    product(1, 0)
    back(1, 0)
    product(1, 1)
    back(1, 1)

    def left_here(part, semaphore):
        pltpu.make_async_copy(part, part, semaphore).wait()

    left_here(x_tx.at[:, :, pl.ds(0, 15)], x_send)
    left_here(l_all.at[:, :, pl.ds(0, 7)], l_send)
    left_here(r_all.at[:, pl.ds(0, 7)], r_send)

    @pl.when(y_lo != y_hi)
    def _():
        left_here(r_all.at[:, pl.ds(0, 1)], r_send)

    left_here(t_tx, t_send)
    left_here(f_rx.at[pl.ds(0, 15)], f_send)

    pltpu.make_async_copy(f_rx, f_rx, f_recv).wait()
    values = finish(
        f_rx[...].reshape(512, 128), off_s[...], gain_s[...], bias_s[...], wide_s[...], out_b[...], roll
    )
    for q in range(4):
        update = values[q] * gate_s[q * 128 : (q + 1) * 128]
        out_ref[4 * q : 4 * q + 4] = update.astype(BF16).reshape(4, 32, 128)


def per_device(*args):
    args = [a.reshape(1, -1) if a.ndim == 1 else a for a in args]
    dma = pltpu.SemaphoreType.DMA
    return pl.pallas_call(
        kernel,
        out_shape=jax.ShapeDtypeStruct(args[0].shape, BF16),
        in_specs=[pl.BlockSpec(memory_space=pl.ANY)] * N_IN,
        out_specs=pl.BlockSpec(memory_space=pltpu.VMEM),
        scratch_shapes=[pltpu.VMEM(a.shape, a.dtype) for a in args]
        + [
            pltpu.VMEM((2, 2, 16, 16, 128), BF16),
            pltpu.VMEM((2, 2, 16, 16, 128), BF16),
            pltpu.VMEM((2, 2, 8, 4, 32, 128), BF16),
            pltpu.VMEM((2, 4, 2, 32, 128), BF16),
            pltpu.VMEM((2, 8, 2, 32, 128), BF16),
            pltpu.VMEM((2, 2, 128, 128), F32),
            pltpu.VMEM((2, 2, 128, 128), F32),
            pltpu.VMEM((2, 2, 128, 128), F32),
            pltpu.VMEM((16, 2, 16, 128), BF16),
            pltpu.VMEM((16, 2, 16, 128), BF16),
            pltpu.VMEM((512, 128), F32),
            pltpu.VMEM((1024, 256), BF16),
            pltpu.VMEM((512, 512), BF16),
            pltpu.VMEM((512, 128), F32),
            pltpu.VMEM((512, 128), F32),
            pltpu.VMEM((512, 128), F32),
            dma((N_IN,)), dma, dma((6,)), dma, dma((2, 2)), dma, dma((2,)), dma, dma((2, 2)), dma, dma,
        ],
        compiler_params=pltpu.CompilerParams(
            collective_id=0, has_side_effects=True, vmem_limit_bytes=40 * 1024 * 1024
        ),
    )(*[pltpu.with_memory_space_constraint(a, pltpu.HBM) for a in args])


def solution(mesh):
    return jax.shard_map(
        per_device,
        mesh=mesh,
        in_specs=(P("row", "col", None), P(), P(), P(), P(), P(), P(), P(), P(), P(), P()),
        out_specs=P("row", "col", None),
        check_vma=False,
    )
```
